32 devices in a mesh: rep: 4 (over y, x), shard: 8 (over z, core).
Axes of the slice: x: 2, y: 2, z: 4, core: 2. Of those that a mesh axis runs over, the one named last changes fastest.
Arguments:
- tokens: bfloat16 [32768, 768], P(('rep', 'shard')), may hold values from -6 to 6
- cotangent: bfloat16 [32768, 768], P(('rep', 'shard')), may hold values from -6 to 6
- seq_lengths: int32 [128], P(('rep', 'shard')), may hold values from 0 to 1024, as said below
- seq_blocks: int32 [128], P(('rep', 'shard')), may hold values from 0 to 8, as said below
- ln1_gain: bfloat16 [768], P('shard'), may hold values from 0.25 to 1.75
- ln1_bias: bfloat16 [768], P('shard'), may hold values from -3 to 3
- w_qkv: bfloat16 [768, 2304], P('shard'), may hold values from -0.21875 to 0.21875
- q_bias: bfloat16 [768], P('shard'), may hold values from -3 to 3
- v_bias: bfloat16 [768], P('shard'), may hold values from -3 to 3
- w_out: bfloat16 [768, 768], P('shard'), may hold values from -0.875 to 0.875
- out_bias: bfloat16 [768], P('shard'), may hold values from -3 to 3
- ln2_gain: bfloat16 [768], P('shard'), may hold values from 0.25 to 1.75
- ln2_bias: bfloat16 [768], P('shard'), may hold values from -3 to 3
- w_fc: bfloat16 [768, 3072], P('shard'), may hold values from -0.21875 to 0.21875
- fc_bias: bfloat16 [3072], P('shard'), may hold values from -3 to 3
- w_proj: bfloat16 [3072, 768], P('shard'), may hold values from -0.15625 to 0.15625
- proj_bias: bfloat16 [768], P('shard'), may hold values from -3 to 3
Outputs:
- output: bfloat16 [32768, 768], P(('rep', 'shard'))
- token_grad: bfloat16 [32768, 768], P(('rep', 'shard'))
- ln1_gain_grad: float32 [768], P('shard')
- ln1_bias_grad: float32 [768], P('shard')
- w_qkv_grad: float32 [768, 2304], P('shard')
- q_bias_grad: float32 [768], P('shard')
- v_bias_grad: float32 [768], P('shard')
- w_out_grad: float32 [768, 768], P('shard')
- out_bias_grad: float32 [768], P('shard')
- ln2_gain_grad: float32 [768], P('shard')
- ln2_bias_grad: float32 [768], P('shard')
- w_fc_grad: float32 [768, 3072], P('shard')
- fc_bias_grad: float32 [3072], P('shard')
- w_proj_grad: float32 [3072, 768], P('shard')
- proj_bias_grad: float32 [768], P('shard')
The draws below stay inside these ranges and needn't reach their ends.
Inputs may be any that keep to these rules, and one draw needn't show every extreme that they name: `seq_lengths`: entries come in groups of 4, one group a device in the order of its index along rep+shard. Slot lengths are 0 for empty slots; a slot's tokens start at 128 times its entry of seq_blocks, the slots of a device follow each other without intersection and stay within its 1024 tokens. In every draw some device holds one sequence of 1024 tokens. `seq_blocks`: block offsets of a device's slots never fall; an empty slot's offset equals the end of the slots before it.
All inputs are finite; a program needn't handle non-finite values.
Results may differ from the reference program's by a relative error of at most 0.015.
Values may be sent and summed in bfloat16 or wider, within the bound.
No kernel may reach another device: no remote copies, remote signals or barrier semaphores. Data moves between devices by JAX's collectives and lax.ppermute only.
A program may use at most 256 MiB of HBM per device.

```python
import jax
import jax.numpy as jnp
from jax import lax

D = 768
HEADS = 12
HEAD_DIM = 64
FF = 3072
TOK_DEV = 1024
SEQ_DEV = 4
BLOCK = 128
TOKENS = 32768
SEQS = 128


def layout(key):
    devices = SEQS // SEQ_DEV
    blocks = TOK_DEV // BLOCK
    k_used, k_share, k_lead, k_full, k_trim = jax.random.split(key, 5)
    used_blocks = jax.random.randint(k_used, (devices,), (blocks + 1) // 2, blocks + 1)
    fuller = jax.random.randint(k_full, (), 0, devices)
    is_full = jnp.arange(devices) == fuller
    used_blocks = jnp.where(is_full, blocks, used_blocks)
    shares = jax.random.randint(k_share, (devices, SEQ_DEV), 0, 4)
    leading = jax.random.randint(k_lead, (devices,), 1, 4)
    shares = shares.at[:, 0].set(leading)
    first_only = (jnp.arange(SEQ_DEV) == 0).astype(jnp.int32)
    shares = jnp.where(is_full[:, None], first_only[None, :], shares)
    portion = used_blocks[:, None] * shares // jnp.sum(shares, axis=1, keepdims=True)
    portion = portion.at[:, 0].add(used_blocks - jnp.sum(portion, axis=1))
    starts = jnp.cumsum(portion, axis=1) - portion
    trimmed = jax.random.randint(k_trim, (devices, SEQ_DEV), 0, BLOCK)
    trimmed = jnp.where(is_full[:, None], 0, trimmed)
    lengths = jnp.where(portion > 0, portion * BLOCK - trimmed, 0)
    return (lengths.reshape(-1).astype(jnp.int32), starts.reshape(-1).astype(jnp.int32))


def draw_seq_lengths(key, part):
    shared = layout(key)
    return shared[0]


def draw_seq_blocks(key, part):
    shared = layout(key)
    return shared[1]


def levels(key, extent, cuts, least, largest):
    gain, own = 1.0, jax.random.fold_in(key, 6)
    for dim, shards_of in cuts:
        heights = jnp.exp(jax.random.uniform(jax.random.fold_in(own, dim), (shards_of,), jnp.float32, least / len(cuts), largest / len(cuts)))
        gain = gain * jnp.repeat(heights, extent[dim] // shards_of).reshape([-1 if axis == dim else 1 for axis in range(len(extent))])
    return gain


def normal_values(stream_key, extent, width, reach, pieces=(), kind=jnp.bfloat16):
    array = jax.random.normal(stream_key, extent, jnp.float32) * width
    if len(pieces) > 0:
        array = levels(stream_key, extent, pieces, -0.22, 0.18) * array
    return jnp.clip(array, min=-reach, max=reach).astype(kind)


def setup_inputs(seed: int = 0) -> dict:
    seeds = jax.random.split(jax.random.key(seed), 18)
    tokens = normal_values(seeds[0], (TOKENS, D), 1.0, 6.0, ((0, 32),))
    cotangent = normal_values(seeds[1], (TOKENS, D), 1.0, 6.0, ((0, 32),))
    seq_lengths = draw_seq_lengths(jax.random.fold_in(seeds[17], 71), 0)
    seq_blocks = draw_seq_blocks(jax.random.fold_in(seeds[17], 71), 0)
    ln1_gain = jnp.clip(1.0 + 0.15 * jax.random.normal(seeds[4], (D,), jnp.float32), 0.25, 1.75).astype(jnp.bfloat16)
    ln1_bias = normal_values(seeds[5], (D,), 0.5, 3.0, ((0, 8),))
    w_qkv = normal_values(seeds[6], (D, 3 * D), D ** -0.5, 0.21875, ((0, 8),))
    q_bias = normal_values(seeds[7], (D,), 0.5, 3.0, ((0, 8),))
    v_bias = normal_values(seeds[8], (D,), 0.5, 3.0, ((0, 8),))
    w_out = normal_values(seeds[9], (D, D), (D // 16) ** -0.5, 0.875, ((0, 8),))
    out_bias = normal_values(seeds[10], (D,), 0.5, 3.0, ((0, 8),))
    ln2_gain = jnp.clip(1.0 + 0.15 * jax.random.normal(seeds[11], (D,), jnp.float32), 0.25, 1.75).astype(jnp.bfloat16)
    ln2_bias = normal_values(seeds[12], (D,), 0.5, 3.0, ((0, 8),))
    w_fc = normal_values(seeds[13], (D, FF), D ** -0.5, 0.21875, ((0, 8),))
    fc_bias = normal_values(seeds[14], (FF,), 0.5, 3.0, ((0, 8),))
    w_proj = normal_values(seeds[15], (FF, D), (FF // 2) ** -0.5, 0.15625, ((0, 8),))
    proj_bias = normal_values(seeds[16], (D,), 0.5, 3.0, ((0, 8),))
    return dict(tokens=tokens, cotangent=cotangent, seq_lengths=seq_lengths, seq_blocks=seq_blocks, ln1_gain=ln1_gain, ln1_bias=ln1_bias, w_qkv=w_qkv, q_bias=q_bias, v_bias=v_bias, w_out=w_out, out_bias=out_bias, ln2_gain=ln2_gain, ln2_bias=ln2_bias, w_fc=w_fc, fc_bias=fc_bias, w_proj=w_proj, proj_bias=proj_bias)


HIGHEST = lax.Precision.HIGHEST

@jax.custom_vjp
def low(v):
    return lax.optimization_barrier(v.astype(jnp.bfloat16)).astype(jnp.float32)

@jax.custom_vjp
def low_back(v):
    return v

def low_keep(v):
    return (low(v), None)

def low_pass(kept, grad):
    return (grad,)

def back_keep(v):
    return (v, None)

def back_low(kept, grad):
    return (low(grad),)
low.defvjp(low_keep, low_pass)
low_back.defvjp(back_keep, back_low)

def layer_norm(values, gain_vec, bias_vec):
    average = lax.optimization_barrier(jnp.mean(values, axis=-1, keepdims=True))
    centred = values - average
    variance = lax.optimization_barrier(jnp.mean(centred * centred, axis=-1, keepdims=True))
    return centred * lax.rsqrt(variance + 1e-05) * gain_vec + bias_vec

def segments(lengths, offsets):
    positions = jnp.arange(TOK_DEV, dtype=jnp.int32)
    starts_at = offsets.astype(jnp.int32) * BLOCK
    ends_at = starts_at + lengths.astype(jnp.int32)
    inside = (positions[None, :] >= starts_at[:, None]) & (positions[None, :] < ends_at[:, None])
    slot_ids = jnp.arange(lengths.shape[0], dtype=jnp.int32)
    seg_ids = lax.optimization_barrier(jnp.sum(jnp.where(inside, slot_ids[:, None], 0), axis=0)).astype(jnp.int32)
    live_mask = jnp.any(inside, axis=0)
    seg_ids = jnp.where(live_mask, seg_ids, -1 - positions)
    return (seg_ids, live_mask)

def attend_device(pair):
    qkv_rows, seg_ids = pair
    rows_here = qkv_rows.shape[0]
    queries = qkv_rows[:, :D].reshape(rows_here, HEADS, HEAD_DIM)
    keys_all = qkv_rows[:, D:2 * D].reshape(rows_here, HEADS, HEAD_DIM)
    values_all = qkv_rows[:, 2 * D:].reshape(rows_here, HEADS, HEAD_DIM)
    factor = float(HEAD_DIM) ** (-0.5)
    scores = jnp.einsum('qhd,khd->hqk', queries, keys_all, precision=HIGHEST) * factor
    scores = low_back(scores)
    positions = jnp.arange(rows_here, dtype=jnp.int32)
    allowed = (seg_ids[:, None] == seg_ids[None, :]) & (positions[None, :] <= positions[:, None])
    scores = jnp.where(allowed[None], scores, -1e+30)
    weights_low = low(jax.nn.softmax(scores, axis=-1))
    mixed_rows = jnp.einsum('hqk,khd->qhd', weights_low, values_all, precision=HIGHEST)
    return mixed_rows.reshape(rows_here, D)

def reference(tokens, cotangent, seq_lengths, seq_blocks, ln1_gain, ln1_bias, w_qkv, q_bias, v_bias, w_out, out_bias, ln2_gain, ln2_bias, w_fc, fc_bias, w_proj, proj_bias):
    device_count = tokens.shape[0] // TOK_DEV
    seg_all, live_all = jax.vmap(segments)(seq_lengths.reshape(device_count, SEQ_DEV), seq_blocks.reshape(device_count, SEQ_DEV))

    def forward(inputs_f, gain_one, bias_one, qkv_weight, query_shift, value_shift, out_weight, out_shift, gain_two, bias_two, fc_weight, fc_shift, proj_weight, proj_shift):
        h_one = low(layer_norm(inputs_f, gain_one, bias_one))
        qkv_shift = jnp.concatenate([query_shift, jnp.zeros((D,), jnp.float32), value_shift])
        qkv_all = low(low_back(jnp.dot(h_one, qkv_weight, precision=HIGHEST) + qkv_shift))
        mixed_all = lax.map(jax.checkpoint(attend_device), (qkv_all.reshape(device_count, TOK_DEV, 3 * D), seg_all))
        attn_low = low(low_back(mixed_all.reshape(-1, D)))
        branch = low_back(jnp.dot(attn_low, out_weight, precision=HIGHEST) + out_shift)
        residual = inputs_f + branch
        h_two = low(layer_norm(residual, gain_two, bias_two))
        pre_act = low_back(jnp.dot(h_two, fc_weight, precision=HIGHEST) + fc_shift)
        act_low = low(jax.nn.gelu(pre_act, approximate=True))
        mlp_out = low_back(jnp.dot(act_low, proj_weight, precision=HIGHEST) + proj_shift)
        return residual + mlp_out
    primals = [tokens, ln1_gain, ln1_bias, w_qkv, q_bias, v_bias, w_out, out_bias, ln2_gain, ln2_bias, w_fc, fc_bias, w_proj, proj_bias]
    primals = [entry.astype(jnp.float32) for entry in primals]
    output, pullback = jax.vjp(forward, primals[0], primals[1], primals[2], primals[3], primals[4], primals[5], primals[6], primals[7], primals[8], primals[9], primals[10], primals[11], primals[12], primals[13])
    upstream = cotangent.astype(jnp.float32) * live_all.reshape(-1)[:, None].astype(jnp.float32)
    grads = pullback(upstream)
    return (output.astype(jnp.bfloat16), grads[0].astype(jnp.bfloat16), grads[1], grads[2], grads[3], grads[4], grads[5], grads[6], grads[7], grads[8], grads[9], grads[10], grads[11], grads[12], grads[13])
```

```python
import functools

import jax
import jax.numpy as jnp
from jax import lax
from jax.experimental import pallas as pl
from jax.experimental.pallas import tpu as pltpu
from jax.sharding import PartitionSpec as P

HEADS = 12
HEAD_DIM = 64
BLOCK = 128
PAIR = 2 * HEAD_DIM
ROWS = 256
MASKED = -1e30
MIB = 1 << 20
F32 = jnp.float32
BF16 = jnp.bfloat16


def dot(left, right):
    return lax.dot_general(left, right, (((1,), (0,)), ((), ())), preferred_element_type=F32)


def dot_nt(left, right):
    return lax.dot_general(left, right, (((1,), (1,)), ((), ())), preferred_element_type=F32)


def dot_tn(left, right):
    return lax.dot_general(left, right, (((0,), (0,)), ((), ())), preferred_element_type=F32)


def normalise(values):
    average = jnp.mean(values, axis=-1, keepdims=True)
    centred = values - average
    variance = jnp.mean(centred * centred, axis=-1, keepdims=True)
    scale = lax.rsqrt(variance + 1e-05)
    return centred * scale, scale


def normalise_back(back_hat, hat, scale):
    inner = jnp.mean(back_hat * hat, axis=-1, keepdims=True)
    return scale * (back_hat - jnp.mean(back_hat, axis=-1, keepdims=True) - hat * inner)


def live_rows(lengths_ref, blocks_ref, first_row, shape):
    rows = first_row + lax.broadcasted_iota(jnp.int32, shape, 0)
    live = None
    for slot in range(lengths_ref.shape[0]):
        start = blocks_ref[slot] * BLOCK
        inside = (rows >= start) & (rows < start + lengths_ref[slot])
        live = inside if live is None else live | inside
    return live


def const_spec(shape):
    return pl.BlockSpec(shape, lambda *_: (0,) * len(shape), pipeline_mode=pl.Buffered(1))


def smem_spec():
    return pl.BlockSpec(memory_space=pltpu.SMEM)


def params(mib):
    return pltpu.CompilerParams(vmem_limit_bytes=mib * MIB, dimension_semantics=("arbitrary",))


def qkv_kernel(x_ref, gain_ref, bias_ref, shift_ref, w_ref, h_ref, qkv_ref):
    hat, _ = normalise(x_ref[...].astype(F32))
    h_one = (hat * gain_ref[...] + bias_ref[...]).astype(BF16)
    h_ref[...] = h_one
    width = x_ref.shape[1]
    for part in range(3):
        cols = slice(part * width, (part + 1) * width)
        out = (dot(h_one, w_ref[:, cols]) + shift_ref[:, cols]).astype(BF16)
        if part == 0:
            out = out * BF16(HEAD_DIM**-0.5)
        qkv_ref[:, cols] = out


def project_qkv(x, gain, bias, shift, w):
    rows, width = x.shape
    wide = w.shape[1]
    return pl.pallas_call(
        qkv_kernel,
        grid=(rows // ROWS,),
        in_specs=[
            pl.BlockSpec((ROWS, width), lambda i: (i, 0)),
            const_spec((1, width)),
            const_spec((1, width)),
            const_spec((1, wide)),
            const_spec((width, wide)),
        ],
        out_specs=[
            pl.BlockSpec((ROWS, width), lambda i: (i, 0)),
            pl.BlockSpec((ROWS, wide), lambda i: (i, 0)),
        ],
        out_shape=[
            jax.ShapeDtypeStruct((rows, width), BF16),
            jax.ShapeDtypeStruct((rows, wide), BF16),
        ],
        compiler_params=params(40),
        cost_estimate=pl.CostEstimate(
            flops=2 * rows * width * wide, bytes_accessed=2 * width * wide + 10 * rows * width, transcendentals=rows
        ),
        name="ln1_qkv",
    )(x, gain, bias, shift, w)


def segment_lanes(lengths_ref, blocks_ref, penalty_ref, member_ref):
    rows = penalty_ref.shape[0]
    shape = (rows, PAIR)
    first = lax.broadcasted_iota(jnp.int32, shape, 0) & ~(BLOCK - 1)
    lane = lax.broadcasted_iota(jnp.int32, shape, 1) & (HEAD_DIM - 1)
    slots = lengths_ref.shape[0]
    member = jnp.full(shape, slots, jnp.int32)
    for slot in range(slots):
        start = blocks_ref[slot] * BLOCK
        inside = (first >= start) & (first < start + lengths_ref[slot])
        member = jnp.where(inside, slot, member)
    same = member == lane
    member_ref[...] = jnp.where(same, 1.0, 0.0).astype(BF16)
    penalty_ref[...] = jnp.where(same | (lane > slots), 0.0, MASKED).astype(BF16)


def low_lanes(rows):
    return lax.broadcasted_iota(jnp.int32, (rows, PAIR), 1) < HEAD_DIM


def attend_kernel(
    lengths_ref, blocks_ref, q_ref, k_ref, v_ref, out_ref, log_ref, penalty_ref, member_ref, key_ref, value_ref
):
    rows = q_ref.shape[0]

    @pl.when(pl.program_id(0) == 0)
    def _():
        segment_lanes(lengths_ref, blocks_ref, penalty_ref, member_ref)

    low = low_lanes(rows)
    one = jnp.ones((), BF16)
    key_ref[0] = jnp.where(low, k_ref[...], member_ref[...])
    key_ref[1] = jnp.where(low, member_ref[...], k_ref[...])
    value_ref[0] = jnp.where(low, v_ref[...], one)
    value_ref[1] = jnp.where(low, one, v_ref[...])
    low = low_lanes(ROWS)
    causal = lax.broadcasted_iota(jnp.int32, (ROWS, ROWS), 1) <= lax.broadcasted_iota(jnp.int32, (ROWS, ROWS), 0)
    for block in range(rows // ROWS):
        here = slice(block * ROWS, (block + 1) * ROWS)
        before = slice(0, block * ROWS)
        q, penalty = q_ref[here], penalty_ref[here]
        mixed, logs = [], []
        for head in range(2):
            q_head = jnp.where(low, q, penalty) if head == 0 else jnp.where(low, penalty, q)
            near = jnp.where(causal, dot_nt(q_head, key_ref[head, here]), MASKED)
            largest = jnp.max(near, axis=-1, keepdims=True)
            if block:
                far = dot_nt(q_head, key_ref[head, before])
                largest = jnp.maximum(largest, jnp.max(far, axis=-1, keepdims=True))
            total = dot(jnp.exp(near - largest).astype(BF16), value_ref[head, here])
            if block:
                total = total + dot(jnp.exp(far - largest).astype(BF16), value_ref[head, before])
            weight = pltpu.roll(total, HEAD_DIM, 1)
            mixed.append(total / weight)
            logs.append(largest + jnp.log(weight))
        out = jnp.where(low, mixed[0], mixed[1]).astype(BF16)
        live = live_rows(lengths_ref, blocks_ref, block * ROWS, (ROWS, PAIR))
        out_ref[here] = jnp.where(live, out, v_ref[here])
        turned = jnp.where(low, logs[0], logs[1]).T
        log_ref[0, 0:1, here] = turned[0:1]
        log_ref[0, 1:2, here] = turned[HEAD_DIM : HEAD_DIM + 1]


def attend(lengths, blocks, qkv):
    rows = qkv.shape[0]
    width = qkv.shape[1] // 3
    pairs = width // PAIR
    return pl.pallas_call(
        attend_kernel,
        grid=(pairs,),
        in_specs=[
            smem_spec(),
            smem_spec(),
            pl.BlockSpec((rows, PAIR), lambda i: (0, i)),
            pl.BlockSpec((rows, PAIR), lambda i: (0, pairs + i)),
            pl.BlockSpec((rows, PAIR), lambda i: (0, 2 * pairs + i)),
        ],
        out_specs=[
            pl.BlockSpec((rows, PAIR), lambda i: (0, i)),
            pl.BlockSpec((1, 2, rows), lambda i: (i, 0, 0)),
        ],
        out_shape=[
            jax.ShapeDtypeStruct((rows, width), BF16),
            jax.ShapeDtypeStruct((pairs, 2, rows), F32),
        ],
        scratch_shapes=[
            pltpu.VMEM((rows, PAIR), BF16),
            pltpu.VMEM((rows, PAIR), BF16),
            pltpu.VMEM((2, rows, PAIR), BF16),
            pltpu.VMEM((2, rows, PAIR), BF16),
        ],
        compiler_params=params(40),
        cost_estimate=pl.CostEstimate(
            flops=8 * rows * rows * width, bytes_accessed=8 * rows * width, transcendentals=rows * rows * pairs
        ),
        name="attend",
    )(lengths, blocks, qkv, qkv, qkv)


def attend_back_kernel(
    lengths_ref,
    blocks_ref,
    q_ref,
    k_ref,
    v_ref,
    out_ref,
    back_ref,
    log_ref,
    grad_ref,
    sums_ref,
    penalty_ref,
    member_ref,
    q_seg,
    q_own,
    back_own,
    q_grad,
):
    rows = q_ref.shape[0]

    @pl.when(pl.program_id(0) == 0)
    def _():
        segment_lanes(lengths_ref, blocks_ref, penalty_ref, member_ref)

    low = low_lanes(rows)
    zero = jnp.zeros((), BF16)
    q, back, penalty = q_ref[...], back_ref[...], penalty_ref[...]
    q_seg[0] = jnp.where(low, q, penalty)
    q_seg[1] = jnp.where(low, penalty, q)
    q_own[0] = jnp.where(low, q, zero)
    q_own[1] = jnp.where(low, zero, q)
    back_own[0] = jnp.where(low, back, zero)
    back_own[1] = jnp.where(low, zero, back)
    inner = (back.astype(F32) * out_ref[...].astype(F32)).T
    inner = [jnp.sum(inner[:HEAD_DIM], axis=0, keepdims=True), jnp.sum(inner[HEAD_DIM:], axis=0, keepdims=True)]
    q_grad[...] = jnp.zeros_like(q_grad)
    low = low_lanes(ROWS)
    causal = lax.broadcasted_iota(jnp.int32, (ROWS, ROWS), 0) <= lax.broadcasted_iota(jnp.int32, (ROWS, ROWS), 1)
    value_sum = jnp.zeros((1, PAIR), F32)
    for block in range(rows // ROWS):
        here = slice(block * ROWS, (block + 1) * ROWS)
        after = slice((block + 1) * ROWS, rows)
        k, v, member = k_ref[here], v_ref[here], member_ref[here]
        key_grad = jnp.zeros((ROWS, PAIR), F32)
        value_grad = jnp.zeros((ROWS, PAIR), F32)
        for head in range(2):
            pick = (lambda a, b: jnp.where(low, a, b)) if head == 0 else (lambda a, b: jnp.where(low, b, a))
            k_seg, k_own, v_own = pick(k, member), pick(k, zero), pick(v, zero)
            for cols in (here, after):
                if cols.start == cols.stop:
                    continue
                prob = jnp.exp(dot_nt(k_seg, q_seg[head, cols]) - log_ref[0, head : head + 1, cols])
                if cols is here:
                    prob = jnp.where(causal, prob, 0.0)
                back_prob = dot_nt(v_own, back_ref[cols])
                back_scores = (prob * (back_prob - inner[head][:, cols])).astype(BF16)
                value_grad = value_grad + dot(prob.astype(BF16), back_own[head, cols])
                key_grad = key_grad + dot(back_scores, q_own[head, cols])
                q_grad[cols] += dot_tn(back_scores, k_own)
        key_low, value_low = key_grad.astype(BF16), value_grad.astype(BF16)
        grad_ref[1, here] = key_low
        grad_ref[2, here] = value_low
        value_sum = value_sum + jnp.sum(value_low.astype(F32), axis=0, keepdims=True)
    q_low = (q_grad[...] * (HEAD_DIM**-0.5)).astype(BF16)
    grad_ref[0] = q_low
    sums_ref[0, 0:1] = jnp.sum(q_low.astype(F32), axis=0, keepdims=True)
    sums_ref[0, 1:2] = value_sum


def attend_back(lengths, blocks, qkv, attn, back_attn, logs):
    rows, width = attn.shape
    pairs = width // PAIR
    own = pl.BlockSpec((rows, PAIR), lambda i: (0, i))
    return pl.pallas_call(
        attend_back_kernel,
        grid=(pairs,),
        in_specs=[
            smem_spec(),
            smem_spec(),
            own,
            pl.BlockSpec((rows, PAIR), lambda i: (0, pairs + i)),
            pl.BlockSpec((rows, PAIR), lambda i: (0, 2 * pairs + i)),
            own,
            own,
            pl.BlockSpec((1, 2, rows), lambda i: (i, 0, 0)),
        ],
        out_specs=[
            pl.BlockSpec((3, rows, PAIR), lambda i: (0, 0, i)),
            pl.BlockSpec((1, 2, PAIR), lambda i: (i, 0, 0)),
        ],
        out_shape=[
            jax.ShapeDtypeStruct((3, rows, width), BF16),
            jax.ShapeDtypeStruct((pairs, 2, PAIR), F32),
        ],
        scratch_shapes=[
            pltpu.VMEM((rows, PAIR), BF16),
            pltpu.VMEM((rows, PAIR), BF16),
            pltpu.VMEM((2, rows, PAIR), BF16),
            pltpu.VMEM((2, rows, PAIR), BF16),
            pltpu.VMEM((2, rows, PAIR), BF16),
            pltpu.VMEM((rows, PAIR), F32),
        ],
        compiler_params=params(48),
        cost_estimate=pl.CostEstimate(
            flops=20 * rows * rows * width, bytes_accessed=16 * rows * width, transcendentals=rows * rows * pairs
        ),
        name="attend_back",
    )(lengths, blocks, qkv, qkv, qkv, attn, back_attn, logs)


def mlp_kernel(
    lengths_ref,
    blocks_ref,
    x_ref,
    attn_ref,
    cot_ref,
    out_bias_ref,
    gain_ref,
    bias_ref,
    fc_bias_ref,
    proj_bias_ref,
    w_out_ref,
    w_fc_ref,
    w_proj_ref,
    output_ref,
    h_ref,
    act_ref,
    back_mlp_ref,
    back_pre_ref,
    back_resid_ref,
    back_branch_ref,
    back_attn_ref,
    sums_ref,
    fc_sums_ref,
):
    step = pl.program_id(0)
    rows, width = x_ref.shape
    hidden = w_fc_ref.shape[1]

    @pl.when(step == 0)
    def _():
        sums_ref[...] = jnp.zeros_like(sums_ref)
        fc_sums_ref[...] = jnp.zeros_like(fc_sums_ref)

    resid = x_ref[...].astype(F32) + dot(attn_ref[...], w_out_ref[...]) + out_bias_ref[...]
    hat, scale = normalise(resid)
    gain = gain_ref[...]
    h_two = (hat * gain + bias_ref[...]).astype(BF16)
    h_ref[...] = h_two
    live = live_rows(lengths_ref, blocks_ref, step * rows, (rows, width))
    back_mlp = jnp.where(live, cot_ref[...], jnp.zeros((), BF16))
    back_mlp_ref[...] = back_mlp
    upstream = back_mlp.astype(F32)
    mlp = jnp.zeros((rows, width), F32)
    back_h = jnp.zeros((rows, width), F32)
    for first in range(0, hidden, width):
        cols = slice(first, first + width)
        pre = dot(h_two, w_fc_ref[:, cols]) + fc_bias_ref[:, cols]
        square = pre * pre
        bent = jnp.tanh(0.7978845608028654 * (pre + 0.044715 * (square * pre)))
        half = 0.5 * (1.0 + bent)
        act = (pre * half).astype(BF16)
        act_ref[:, cols] = act
        slope = half + 0.5 * pre * (1.0 - bent * bent) * (0.7978845608028654 + 0.1070322242 * square)
        mlp = mlp + dot(act, w_proj_ref[cols])
        back_pre = (dot_nt(back_mlp, w_proj_ref[cols]) * slope).astype(BF16)
        back_pre_ref[:, cols] = back_pre
        fc_sums_ref[:, cols] += jnp.sum(back_pre.astype(F32), axis=0, keepdims=True)
        back_h = back_h + dot_nt(back_pre, w_fc_ref[:, cols])
    output_ref[...] = (resid + mlp + proj_bias_ref[...]).astype(BF16)
    back_resid = upstream + normalise_back(back_h * gain, hat, scale)
    back_resid_ref[...] = back_resid
    back_branch = back_resid.astype(BF16)
    back_branch_ref[...] = back_branch
    back_attn_ref[...] = dot_nt(back_branch, w_out_ref[...]).astype(BF16)
    sums_ref[0:1] += jnp.sum(back_h * hat, axis=0, keepdims=True)
    sums_ref[1:2] += jnp.sum(back_h, axis=0, keepdims=True)
    sums_ref[2:3] += jnp.sum(upstream, axis=0, keepdims=True)
    sums_ref[3:4] += jnp.sum(back_branch.astype(F32), axis=0, keepdims=True)


def mlp_both_ways(lengths, blocks, x, attn, cot, out_bias, gain, bias, fc_bias, proj_bias, w_out, w_fc, w_proj):
    rows, width = x.shape
    hidden = w_fc.shape[1]
    tile = pl.BlockSpec((ROWS, width), lambda i: (i, 0))
    wide = pl.BlockSpec((ROWS, hidden), lambda i: (i, 0))
    vec = const_spec((1, width))

    def shaped(cols, kind):
        return jax.ShapeDtypeStruct((rows, cols), kind)

    return pl.pallas_call(
        mlp_kernel,
        grid=(rows // ROWS,),
        in_specs=[smem_spec(), smem_spec(), tile, tile, tile, vec, vec, vec, const_spec((1, hidden)), vec]
        + [const_spec(w_out.shape), const_spec(w_fc.shape), const_spec(w_proj.shape)],
        out_specs=[tile, tile, wide, tile, wide, tile, tile, tile]
        + [pl.BlockSpec((8, width), lambda i: (0, 0)), pl.BlockSpec((1, hidden), lambda i: (0, 0))],
        out_shape=[
            shaped(width, BF16),
            shaped(width, BF16),
            shaped(hidden, BF16),
            shaped(width, BF16),
            shaped(hidden, BF16),
            shaped(width, F32),
            shaped(width, BF16),
            shaped(width, BF16),
            jax.ShapeDtypeStruct((8, width), F32),
            jax.ShapeDtypeStruct((1, hidden), F32),
        ],
        compiler_params=params(58),
        cost_estimate=pl.CostEstimate(
            flops=4 * rows * width * (width + 2 * hidden),
            bytes_accessed=40 * rows * width,
            transcendentals=rows * hidden,
        ),
        name="mlp",
    )(lengths, blocks, x, attn, cot, out_bias, gain, bias, fc_bias, proj_bias, w_out, w_fc, w_proj)


def tn_kernel(left_ref, right_ref, out_ref):
    out_ref[...] = dot_tn(left_ref[...], right_ref[...].reshape(left_ref.shape[0], -1)).astype(out_ref.dtype)


def weight_grad(left, right, by_left, name):
    rows = left.shape[0]
    unit = 768
    if right.ndim == 3:
        steps, right_spec = right.shape[0], pl.BlockSpec((1, rows, unit), lambda i: (i, 0, 0))
        shape = (left.shape[1], right.shape[0] * unit)
    else:
        steps = max(left.shape[1], right.shape[1]) // unit
        right_spec = pl.BlockSpec((rows, unit), lambda i: (0, 0 if by_left else i))
        shape = (left.shape[1], right.shape[1])
    return pl.pallas_call(
        tn_kernel,
        grid=(steps,),
        in_specs=[pl.BlockSpec((rows, unit), lambda i: (0, i if by_left else 0)), right_spec],
        out_specs=pl.BlockSpec((unit, unit), lambda i: (i, 0) if by_left else (0, i)),
        out_shape=jax.ShapeDtypeStruct(shape, BF16),
        compiler_params=params(40),
        cost_estimate=pl.CostEstimate(
            flops=2 * rows * shape[0] * shape[1], bytes_accessed=2 * shape[0] * shape[1], transcendentals=0
        ),
        name=name,
    )(left, right)


def qkv_back_kernel(x_ref, gain_ref, w_ref, back_ref, resid_ref, out_ref, sums_ref):
    @pl.when(pl.program_id(0) == 0)
    def _():
        sums_ref[...] = jnp.zeros_like(sums_ref)

    width = x_ref.shape[1]
    back_h = dot_nt(back_ref[0], w_ref[:, :width])
    back_h = back_h + dot_nt(back_ref[1], w_ref[:, width : 2 * width])
    back_h = back_h + dot_nt(back_ref[2], w_ref[:, 2 * width :])
    hat, scale = normalise(x_ref[...].astype(F32))
    out_ref[...] = (resid_ref[...] + normalise_back(back_h * gain_ref[...], hat, scale)).astype(BF16)
    sums_ref[0:1] += jnp.sum(back_h * hat, axis=0, keepdims=True)
    sums_ref[1:2] += jnp.sum(back_h, axis=0, keepdims=True)


def qkv_back(x, gain, w, back_qkv, back_resid):
    rows, width = x.shape
    tile = pl.BlockSpec((ROWS, width), lambda i: (i, 0))
    return pl.pallas_call(
        qkv_back_kernel,
        grid=(rows // ROWS,),
        in_specs=[
            tile,
            const_spec((1, width)),
            const_spec(w.shape),
            pl.BlockSpec((3, ROWS, width), lambda i: (0, i, 0)),
            tile,
        ],
        out_specs=[tile, pl.BlockSpec((8, width), lambda i: (0, 0))],
        out_shape=[jax.ShapeDtypeStruct((rows, width), BF16), jax.ShapeDtypeStruct((8, width), F32)],
        compiler_params=params(40),
        cost_estimate=pl.CostEstimate(
            flops=6 * rows * width * width, bytes_accessed=20 * rows * width, transcendentals=rows
        ),
        name="qkv_back",
    )(x, gain, w, back_qkv, back_resid)


def gather(value):
    return lax.all_gather(value, "shard", axis=0, tiled=True)


def spread(value):
    own = lax.psum_scatter(value.astype(BF16), "shard", scatter_dimension=0, tiled=True)
    return lax.psum(own, "rep").astype(F32)


def local(
    tokens,
    cotangent,
    seq_lengths,
    seq_blocks,
    ln1_gain,
    ln1_bias,
    w_qkv,
    q_bias,
    v_bias,
    w_out,
    out_bias,
    ln2_gain,
    ln2_bias,
    w_fc,
    fc_bias,
    w_proj,
    proj_bias,
):
    width = tokens.shape[1]
    small = jnp.concatenate(
        [ln1_gain, ln1_bias, q_bias, v_bias, out_bias, ln2_gain, ln2_bias, proj_bias, fc_bias]
    ).reshape(1, -1)
    own = w_qkv.shape[0]
    small = gather(small).astype(F32)

    def vec(index, count=1):
        return small[:, index * own : (index + count) * own].reshape(1, -1)

    gain_one, bias_one, query_shift, value_shift, out_shift, gain_two, bias_two, proj_shift = (
        vec(index) for index in range(8)
    )
    fc_shift = vec(8, fc_bias.shape[0] // own)
    qkv_shift = jnp.concatenate([query_shift, jnp.zeros_like(query_shift), value_shift], axis=1)
    full_qkv, full_out, full_fc, full_proj = gather(w_qkv), gather(w_out), gather(w_fc), gather(w_proj)
    h_one, qkv = project_qkv(tokens, gain_one, bias_one, qkv_shift, full_qkv)
    attn, logs = attend(seq_lengths, seq_blocks, qkv)
    output, h_two, act, back_mlp, back_pre, back_resid, back_branch, back_attn, mlp_sums, fc_sums = mlp_both_ways(
        seq_lengths,
        seq_blocks,
        tokens,
        attn,
        cotangent,
        out_shift,
        gain_two,
        bias_two,
        fc_shift,
        proj_shift,
        full_out,
        full_fc,
        full_proj,
    )
    grad_proj = weight_grad(act, back_mlp, True, "grad_proj")
    grad_fc = weight_grad(h_two, back_pre, False, "grad_fc")
    grad_out = weight_grad(attn, back_branch, False, "grad_out")
    back_qkv, qkv_sums = attend_back(seq_lengths, seq_blocks, qkv, attn, back_attn, logs)
    grad_qkv = weight_grad(h_one, back_qkv, False, "grad_qkv")
    token_grad, ln_sums = qkv_back(tokens, gain_one, full_qkv, back_qkv, back_resid)
    return (
        output,
        token_grad,
        spread(ln_sums[0]),
        spread(ln_sums[1]),
        spread(grad_qkv),
        spread(qkv_sums[:, 0].reshape(-1)),
        spread(qkv_sums[:, 1].reshape(-1)),
        spread(grad_out),
        spread(mlp_sums[3]),
        spread(mlp_sums[0]),
        spread(mlp_sums[1]),
        spread(grad_fc),
        spread(fc_sums[0]),
        spread(grad_proj),
        spread(mlp_sums[2]),
    )


def solution(mesh):
    both = ("rep", "shard")
    matrix, vector = P("shard", None), P("shard")
    return jax.shard_map(
        local,
        mesh=mesh,
        in_specs=(
            P(both, None),
            P(both, None),
            P(both),
            P(both),
            vector,
            vector,
            matrix,
            vector,
            vector,
            matrix,
            vector,
            vector,
            vector,
            matrix,
            vector,
            matrix,
            vector,
        ),
        out_specs=(
            P(both, None),
            P(both, None),
            vector,
            vector,
            matrix,
            vector,
            vector,
            matrix,
            vector,
            vector,
            vector,
            matrix,
            vector,
            matrix,
            vector,
        ),
        check_vma=False,
    )
```

```python
import functools

import jax
import jax.numpy as jnp
from jax import lax
from jax.experimental import pallas as pl
from jax.experimental.pallas import tpu as pltpu
from jax.sharding import PartitionSpec as P

HEADS = 12
HEAD_DIM = 64
BLOCK = 128
PAIR = 2 * HEAD_DIM
ROWS = 256
MASKED = -1e30
MIB = 1 << 20
F32 = jnp.float32
BF16 = jnp.bfloat16


def dot(left, right):
    return lax.dot_general(left, right, (((1,), (0,)), ((), ())), preferred_element_type=F32)


def dot_nt(left, right):
    return lax.dot_general(left, right, (((1,), (1,)), ((), ())), preferred_element_type=F32)


def dot_tn(left, right):
    return lax.dot_general(left, right, (((0,), (0,)), ((), ())), preferred_element_type=F32)


def normalise(values):
    average = jnp.mean(values, axis=-1, keepdims=True)
    centred = values - average
    variance = jnp.mean(centred * centred, axis=-1, keepdims=True)
    scale = lax.rsqrt(variance + 1e-05)
    return centred * scale, scale


def normalise_back(back_hat, hat, scale):
    inner = jnp.mean(back_hat * hat, axis=-1, keepdims=True)
    return scale * (back_hat - jnp.mean(back_hat, axis=-1, keepdims=True) - hat * inner)


def live_rows(lengths_ref, blocks_ref, first_row, shape):
    rows = first_row + lax.broadcasted_iota(jnp.int32, shape, 0)
    live = None
    for slot in range(lengths_ref.shape[0]):
        start = blocks_ref[slot] * BLOCK
        inside = (rows >= start) & (rows < start + lengths_ref[slot])
        live = inside if live is None else live | inside
    return live


def const_spec(shape):
    return pl.BlockSpec(shape, lambda *_: (0,) * len(shape), pipeline_mode=pl.Buffered(1))


def smem_spec():
    return pl.BlockSpec(memory_space=pltpu.SMEM)


def params(mib):
    return pltpu.CompilerParams(vmem_limit_bytes=mib * MIB, dimension_semantics=("arbitrary",))


def piece_copies(place_ref, target, pieces, sems, by_rows, first_col=0):
    core, plane, across, along = (place_ref[i] for i in range(4))
    shard_rows, cols = pieces[0][0].shape
    if by_rows:
        rows, half = shard_rows // 4, cols
    else:
        rows, half = shard_rows // 2, cols // 2
    copies = []

    def add(source, row, col):
        sem = sems.at[len(copies)]
        copies.append(pltpu.make_async_copy(source, target.at[pl.ds(row, source.shape[0]), col], sem))

    for other_core in range(2):
        own, *quarters = pieces[other_core]
        add(own, pl.multiple_of((plane * 2 + (core ^ other_core)) * shard_rows, 16), slice(None))
        for other_plane in range(1, 4):
            base = ((plane ^ other_plane) * 2 + (core ^ other_core)) * shard_rows
            for quarter in range(4):
                low, high = across ^ (quarter & 1), along ^ (quarter >> 1)
                block = quarters[quarter].at[other_plane - 1]
                if by_rows:
                    add(block, pl.multiple_of(base + (2 * high + low) * rows, 16), slice(None))
                else:
                    source = block.at[:, pl.ds(first_col, half)]
                    column = pl.ds(pl.multiple_of(low * half, 128), half)
                    add(source, pl.multiple_of(base + high * rows, 16), column)
    return copies


PIECES = 10
COPIES = 26


def any_spec():
    return pl.BlockSpec(memory_space=pl.ANY)


def split_pieces(refs):
    return [refs[: PIECES // 2], refs[PIECES // 2 :]]


def qkv_kernel(place_ref, x_ref, table_ref, *refs):
    *pieces, h_ref, qkv_ref, w_ref, sems = refs
    copies = []
    if len(pieces) == PIECES:
        copies = piece_copies(place_ref, w_ref, split_pieces(pieces), sems, False)
    else:
        copies = [pltpu.make_async_copy(pieces[0], w_ref, sems.at[0])]
    first = pl.program_id(0) == 0

    @pl.when(first)
    def _():
        for copy in copies:
            copy.start()

    hat, _ = normalise(x_ref[...].astype(F32))
    h_one = (hat * table_ref[0:1] + table_ref[1:2]).astype(BF16)
    h_ref[...] = h_one
    width = x_ref.shape[1]

    @pl.when(first)
    def _():
        for copy in copies:
            copy.wait()

    for part in range(3):
        cols = slice(part * width, (part + 1) * width)
        out = dot(h_one, w_ref[:, cols])
        if part != 1:
            out = out + table_ref[2 + part // 2 : 3 + part // 2]
        out = out.astype(BF16)
        if part == 0:
            out = out * BF16(HEAD_DIM**-0.5)
        qkv_ref[:, cols] = out


def project_qkv(place, x, table, pieces):
    rows, width = x.shape
    wide = 3 * width
    return pl.pallas_call(
        qkv_kernel,
        grid=(rows // ROWS,),
        in_specs=[
            smem_spec(),
            pl.BlockSpec((ROWS, width), lambda i: (i, 0)),
            const_spec(table.shape),
        ]
        + [any_spec()] * len(pieces),
        out_specs=[
            pl.BlockSpec((ROWS, width), lambda i: (i, 0)),
            pl.BlockSpec((ROWS, wide), lambda i: (i, 0)),
            const_spec((width, wide)),
        ],
        out_shape=[
            jax.ShapeDtypeStruct((rows, width), BF16),
            jax.ShapeDtypeStruct((rows, wide), BF16),
            jax.ShapeDtypeStruct((width, wide), BF16),
        ],
        scratch_shapes=[pltpu.SemaphoreType.DMA((COPIES,))],
        compiler_params=params(60),
        cost_estimate=pl.CostEstimate(
            flops=6 * rows * width * wide, bytes_accessed=2 * width * wide + 10 * rows * width, transcendentals=rows
        ),
        name="ln1_qkv",
    )(place, x, table, *pieces)


def segment_lanes(lengths_ref, blocks_ref, penalty_ref, member_ref):
    rows = penalty_ref.shape[0]
    shape = (rows, PAIR)
    first = lax.broadcasted_iota(jnp.int32, shape, 0) & ~(BLOCK - 1)
    lane = lax.broadcasted_iota(jnp.int32, shape, 1) & (HEAD_DIM - 1)
    slots = lengths_ref.shape[0]
    member = jnp.full(shape, slots, jnp.int32)
    for slot in range(slots):
        start = blocks_ref[slot] * BLOCK
        inside = (first >= start) & (first < start + lengths_ref[slot])
        member = jnp.where(inside, slot, member)
    same = member == lane
    member_ref[...] = jnp.where(same, 1.0, 0.0).astype(BF16)
    penalty_ref[...] = jnp.where(same | (lane > slots), 0.0, MASKED).astype(BF16)


def low_lanes(rows):
    return lax.broadcasted_iota(jnp.int32, (rows, PAIR), 1) < HEAD_DIM


def attend_kernel(
    lengths_ref, blocks_ref, q_ref, k_ref, v_ref, *refs
):
    out_ref, log_ref, penalty_ref, member_ref, key_ref, value_ref = refs[-6:]
    rows = q_ref.shape[0]

    @pl.when(pl.program_id(0) == 0)
    def _():
        segment_lanes(lengths_ref, blocks_ref, penalty_ref, member_ref)

    low = low_lanes(rows)
    one = jnp.ones((), BF16)
    key_ref[0] = jnp.where(low, k_ref[...], member_ref[...])
    key_ref[1] = jnp.where(low, member_ref[...], k_ref[...])
    value_ref[0] = jnp.where(low, v_ref[...], one)
    value_ref[1] = jnp.where(low, one, v_ref[...])
    low = low_lanes(ROWS)
    causal = lax.broadcasted_iota(jnp.int32, (ROWS, ROWS), 1) <= lax.broadcasted_iota(jnp.int32, (ROWS, ROWS), 0)
    for block in range(rows // ROWS):
        here = slice(block * ROWS, (block + 1) * ROWS)
        before = slice(0, block * ROWS)
        q, penalty = q_ref[here], penalty_ref[here]
        mixed, logs = [], []
        for head in range(2):
            q_head = jnp.where(low, q, penalty) if head == 0 else jnp.where(low, penalty, q)
            near = jnp.where(causal, dot_nt(q_head, key_ref[head, here]), MASKED)
            largest = jnp.max(near, axis=-1, keepdims=True)
            if block:
                far = dot_nt(q_head, key_ref[head, before])
                largest = jnp.maximum(largest, jnp.max(far, axis=-1, keepdims=True))
            total = dot(jnp.exp(near - largest).astype(BF16), value_ref[head, here])
            if block:
                total = total + dot(jnp.exp(far - largest).astype(BF16), value_ref[head, before])
            weight = pltpu.roll(total, HEAD_DIM, 1)
            mixed.append(total / weight)
            logs.append(largest + jnp.log(weight))
        out = jnp.where(low, mixed[0], mixed[1]).astype(BF16)
        live = live_rows(lengths_ref, blocks_ref, block * ROWS, (ROWS, PAIR))
        out_ref[here] = jnp.where(live, out, v_ref[here])
        turned = jnp.where(low, logs[0], logs[1]).T
        log_ref[0, 0:1, here] = turned[0:1]
        log_ref[0, 1:2, here] = turned[HEAD_DIM : HEAD_DIM + 1]


def attend(lengths, blocks, qkv, first, count, earlier=()):
    rows = qkv.shape[0]
    width = qkv.shape[1] // 3
    pairs = width // PAIR
    return pl.pallas_call(
        attend_kernel,
        grid=(count,),
        in_specs=[
            smem_spec(),
            smem_spec(),
            pl.BlockSpec((rows, PAIR), lambda i: (0, first + i)),
            pl.BlockSpec((rows, PAIR), lambda i: (0, pairs + first + i)),
            pl.BlockSpec((rows, PAIR), lambda i: (0, 2 * pairs + first + i)),
        ]
        + [any_spec()] * len(earlier),
        out_specs=[
            pl.BlockSpec((rows, PAIR), lambda i: (0, first + i)),
            pl.BlockSpec((1, 2, rows), lambda i: (first + i, 0, 0)),
        ],
        out_shape=[
            jax.ShapeDtypeStruct((rows, width), BF16),
            jax.ShapeDtypeStruct((pairs, 2, rows), F32),
        ],
        scratch_shapes=[
            pltpu.VMEM((rows, PAIR), BF16),
            pltpu.VMEM((rows, PAIR), BF16),
            pltpu.VMEM((2, rows, PAIR), BF16),
            pltpu.VMEM((2, rows, PAIR), BF16),
        ],
        input_output_aliases={5 + i: i for i in range(len(earlier))},
        compiler_params=params(60),
        cost_estimate=pl.CostEstimate(
            flops=38 * rows * rows * count * PAIR,
            bytes_accessed=8 * rows * count * PAIR,
            transcendentals=rows * rows * count,
        ),
        name="attend",
    )(lengths, blocks, qkv, qkv, qkv, *earlier)


def attend_back_kernel(
    lengths_ref,
    blocks_ref,
    q_ref,
    k_ref,
    v_ref,
    out_ref,
    back_ref,
    log_ref,
    *refs,
):
    grad_ref, sums_ref, penalty_ref, member_ref, q_seg, q_own, back_own, q_grad = refs[-8:]
    rows = q_ref.shape[0]

    @pl.when(pl.program_id(0) == 0)
    def _():
        segment_lanes(lengths_ref, blocks_ref, penalty_ref, member_ref)

    low = low_lanes(rows)
    zero = jnp.zeros((), BF16)
    q, back, penalty = q_ref[...], back_ref[...], penalty_ref[...]
    q_seg[0] = jnp.where(low, q, penalty)
    q_seg[1] = jnp.where(low, penalty, q)
    q_own[0] = jnp.where(low, q, zero)
    q_own[1] = jnp.where(low, zero, q)
    back_own[0] = jnp.where(low, back, zero)
    back_own[1] = jnp.where(low, zero, back)
    inner = (back.astype(F32) * out_ref[...].astype(F32)).T
    inner = [jnp.sum(inner[:HEAD_DIM], axis=0, keepdims=True), jnp.sum(inner[HEAD_DIM:], axis=0, keepdims=True)]
    q_grad[...] = jnp.zeros_like(q_grad)
    low = low_lanes(ROWS)
    causal = lax.broadcasted_iota(jnp.int32, (ROWS, ROWS), 0) <= lax.broadcasted_iota(jnp.int32, (ROWS, ROWS), 1)
    value_sum = jnp.zeros((1, PAIR), F32)
    for block in range(rows // ROWS):
        here = slice(block * ROWS, (block + 1) * ROWS)
        after = slice((block + 1) * ROWS, rows)
        k, v, member = k_ref[here], v_ref[here], member_ref[here]
        key_grad = jnp.zeros((ROWS, PAIR), F32)
        value_grad = jnp.zeros((ROWS, PAIR), F32)
        for head in range(2):
            pick = (lambda a, b: jnp.where(low, a, b)) if head == 0 else (lambda a, b: jnp.where(low, b, a))
            k_seg, k_own, v_own = pick(k, member), pick(k, zero), pick(v, zero)
            for cols in (here, after):
                if cols.start == cols.stop:
                    continue
                prob = jnp.exp(dot_nt(k_seg, q_seg[head, cols]) - log_ref[0, head : head + 1, cols])
                if cols is here:
                    prob = jnp.where(causal, prob, 0.0)
                back_prob = dot_nt(v_own, back_ref[cols])
                back_scores = (prob * (back_prob - inner[head][:, cols])).astype(BF16)
                value_grad = value_grad + dot(prob.astype(BF16), back_own[head, cols])
                key_grad = key_grad + dot(back_scores, q_own[head, cols])
                q_grad[cols] += dot_tn(back_scores, k_own)
        key_low, value_low = key_grad.astype(BF16), value_grad.astype(BF16)
        grad_ref[1, here] = key_low
        grad_ref[2, here] = value_low
        value_sum = value_sum + jnp.sum(value_low.astype(F32), axis=0, keepdims=True)
    q_low = (q_grad[...] * (HEAD_DIM**-0.5)).astype(BF16)
    grad_ref[0] = q_low
    sums_ref[0:1] = jnp.sum(q_low.astype(F32), axis=0, keepdims=True)
    sums_ref[1:2] = value_sum


def attend_back(lengths, blocks, qkv, attn, back_attn, logs, first, count, earlier=()):
    rows, width = attn.shape
    pairs = width // PAIR
    own = pl.BlockSpec((rows, PAIR), lambda i: (0, first + i))
    return pl.pallas_call(
        attend_back_kernel,
        grid=(count,),
        in_specs=[
            smem_spec(),
            smem_spec(),
            own,
            pl.BlockSpec((rows, PAIR), lambda i: (0, pairs + first + i)),
            pl.BlockSpec((rows, PAIR), lambda i: (0, 2 * pairs + first + i)),
            own,
            own,
            pl.BlockSpec((1, 2, rows), lambda i: (first + i, 0, 0)),
        ]
        + [any_spec()] * len(earlier),
        out_specs=[
            pl.BlockSpec((3, rows, PAIR), lambda i: (0, 0, first + i)),
            pl.BlockSpec((8, PAIR), lambda i: (0, first + i)),
        ],
        out_shape=[
            jax.ShapeDtypeStruct((3, rows, width), BF16),
            jax.ShapeDtypeStruct((8, width), F32),
        ],
        scratch_shapes=[
            pltpu.VMEM((rows, PAIR), BF16),
            pltpu.VMEM((rows, PAIR), BF16),
            pltpu.VMEM((2, rows, PAIR), BF16),
            pltpu.VMEM((2, rows, PAIR), BF16),
            pltpu.VMEM((2, rows, PAIR), BF16),
            pltpu.VMEM((rows, PAIR), F32),
        ],
        input_output_aliases={8 + i: i for i in range(len(earlier))},
        compiler_params=params(60),
        cost_estimate=pl.CostEstimate(
            flops=49 * rows * rows * count * PAIR,
            bytes_accessed=16 * rows * count * PAIR,
            transcendentals=rows * rows * count,
        ),
        name="attend_back",
    )(lengths, blocks, qkv, qkv, qkv, attn, back_attn, logs, *earlier)


def mlp_kernel(
    place_ref,
    lengths_ref,
    blocks_ref,
    x_ref,
    attn_ref,
    cot_ref,
    table_ref,
    fc_bias_ref,
    *refs,
):
    *pieces, output_ref, h_ref, act_ref, back_mlp_ref, back_pre_ref = refs[:-9]
    back_resid_ref, back_branch_ref, back_attn_ref, sums_ref, fc_sums_ref, w_out_ref, w_fc_ref, w_proj_ref, sems = refs[-9:]
    if len(pieces) == 22:
        wide_pieces = [pieces[:6], pieces[6:12]]
        fc_pieces, out_pieces = ([[core[i], *core[2:]] for core in wide_pieces] for i in range(2))
        out_copies = piece_copies(place_ref, w_out_ref, out_pieces, sems, False, fc_pieces[0][0].shape[1] // 2)
        fc_copies = piece_copies(place_ref, w_fc_ref, fc_pieces, sems.at[pl.ds(COPIES, COPIES)], False)
        proj_copies = piece_copies(
            place_ref, w_proj_ref, split_pieces(pieces[12:]), sems.at[pl.ds(2 * COPIES, COPIES)], True
        )
    else:
        out_copies, fc_copies, proj_copies = (
            [pltpu.make_async_copy(pieces[i], target, sems.at[i])]
            for i, target in enumerate((w_out_ref, w_fc_ref, w_proj_ref))
        )
    first_step = pl.program_id(0) == 0

    @pl.when(first_step)
    def _():
        for copy in out_copies + fc_copies + proj_copies:
            copy.start()
        for copy in out_copies:
            copy.wait()

    step = pl.program_id(0)
    rows, width = x_ref.shape
    hidden = w_fc_ref.shape[1]

    @pl.when(step == 0)
    def _():
        sums_ref[...] = jnp.zeros_like(sums_ref)
        fc_sums_ref[...] = jnp.zeros_like(fc_sums_ref)

    resid = x_ref[...].astype(F32) + dot(attn_ref[...], w_out_ref[...]) + table_ref[4:5]
    hat, scale = normalise(resid)
    gain = table_ref[5:6]
    h_two = (hat * gain + table_ref[6:7]).astype(BF16)
    h_ref[...] = h_two

    @pl.when(first_step)
    def _():
        for copy in fc_copies + proj_copies:
            copy.wait()

    live = live_rows(lengths_ref, blocks_ref, step * rows, (rows, width))
    back_mlp = jnp.where(live, cot_ref[...], jnp.zeros((), BF16))
    back_mlp_ref[...] = back_mlp
    upstream = back_mlp.astype(F32)
    mlp = jnp.zeros((rows, width), F32)
    back_h = jnp.zeros((rows, width), F32)
    for first in range(0, hidden, width):
        cols = slice(first, first + width)
        pre = dot(h_two, w_fc_ref[:, cols]) + fc_bias_ref[:, cols]
        square = pre * pre
        bent = jnp.tanh(0.7978845608028654 * (pre + 0.044715 * (square * pre)))
        half = 0.5 * (1.0 + bent)
        act = (pre * half).astype(BF16)
        act_ref[:, cols] = act
        slope = half + 0.5 * pre * (1.0 - bent * bent) * (0.7978845608028654 + 0.1070322242 * square)
        mlp = mlp + dot(act, w_proj_ref[cols])
        back_pre = (dot_nt(back_mlp, w_proj_ref[cols]) * slope).astype(BF16)
        back_pre_ref[:, cols] = back_pre
        fc_sums_ref[:, cols] += jnp.sum(back_pre.astype(F32), axis=0, keepdims=True)
        back_h = back_h + dot_nt(back_pre, w_fc_ref[:, cols])
    output_ref[...] = (resid + mlp + table_ref[7:8]).astype(BF16)
    back_resid = upstream + normalise_back(back_h * gain, hat, scale)
    back_resid_ref[...] = back_resid
    back_branch = back_resid.astype(BF16)
    back_branch_ref[...] = back_branch
    back_attn_ref[...] = dot_nt(back_branch, w_out_ref[...]).astype(BF16)
    sums_ref[0:1] += jnp.sum(back_h * hat, axis=0, keepdims=True)
    sums_ref[1:2] += jnp.sum(back_h, axis=0, keepdims=True)
    sums_ref[2:3] += jnp.sum(upstream, axis=0, keepdims=True)
    sums_ref[3:4] += jnp.sum(back_branch.astype(F32), axis=0, keepdims=True)


def mlp_both_ways(place, lengths, blocks, x, attn, cot, table, fc_bias, pieces):
    rows, width = x.shape
    hidden = fc_bias.shape[1]
    tile = pl.BlockSpec((ROWS, width), lambda i: (i, 0))
    wide = pl.BlockSpec((ROWS, hidden), lambda i: (i, 0))

    def shaped(cols, kind):
        return jax.ShapeDtypeStruct((rows, cols), kind)

    return pl.pallas_call(
        mlp_kernel,
        grid=(rows // ROWS,),
        in_specs=[smem_spec()] * 3
        + [tile, tile, tile, const_spec(table.shape), const_spec((1, hidden))]
        + [any_spec()] * len(pieces),
        out_specs=[tile, tile, wide, tile, wide, tile, tile, tile]
        + [pl.BlockSpec((8, width), lambda i: (0, 0)), pl.BlockSpec((1, hidden), lambda i: (0, 0))],
        out_shape=[
            shaped(width, BF16),
            shaped(width, BF16),
            shaped(hidden, BF16),
            shaped(width, BF16),
            shaped(hidden, BF16),
            shaped(width, F32),
            shaped(width, BF16),
            shaped(width, BF16),
            jax.ShapeDtypeStruct((8, width), F32),
            jax.ShapeDtypeStruct((1, hidden), F32),
        ],
        scratch_shapes=[
            pltpu.VMEM((width, width), BF16),
            pltpu.VMEM((width, hidden), BF16),
            pltpu.VMEM((hidden, width), BF16),
            pltpu.SemaphoreType.DMA((3 * COPIES,)),
        ],
        compiler_params=params(60),
        cost_estimate=pl.CostEstimate(
            flops=8 * rows * width * (width + 2 * hidden),
            bytes_accessed=40 * rows * width,
            transcendentals=rows * hidden,
        ),
        name="mlp",
    )(place, lengths, blocks, x, attn, cot, table, fc_bias, *pieces)


def split_grad_kernel(place_ref, left_ref, right_ref, keep_ref, send_ref, total):
    core, plane, across, along = (place_ref[i] for i in range(4))
    right = right_ref[...]
    if right.ndim == 3:
        right = jnp.concatenate([right[i] for i in range(right.shape[0])], axis=1)
    total[...] = dot_tn(left_ref[...], right)
    rows = keep_ref.shape[3]
    by_rows = keep_ref.shape[2] == 1
    for to, ref in ((core, keep_ref), (1 - core, send_ref)):
        if by_rows:
            for quarter in range(4):
                source = pl.ds(pl.multiple_of((to * 4 + quarter) * rows, 16), rows)
                ref[along ^ (quarter >> 1), across ^ (quarter & 1), 0] = total[source].astype(BF16)
        else:
            for other in range(4):
                for half in range(2):
                    source = pl.ds(pl.multiple_of(((other * 2 + to) * 2 + half) * rows, 16), rows)
                    ref[along ^ half, 0, plane ^ other] = total[source].astype(BF16)


def wide_grad_kernel(place_ref, h_ref, attn_ref, pre_ref, branch_ref, keep_ref, send_ref, total):
    core, along = place_ref[0], place_ref[3]
    step = pl.program_id(1)
    rows, unit = keep_ref.shape[3], pre_ref.shape[1]

    def emit(first, width):
        for to, ref in ((core, keep_ref), (1 - core, send_ref)):
            for other in range(4):
                for half in range(2):
                    source = pl.ds(pl.multiple_of(((other * 2 + to) * 2 + half) * rows, 16), rows)
                    ref[along ^ half, 0, other, :, first : first + width] = total[source, :width].astype(BF16)

    total[...] = dot_tn(h_ref[...], pre_ref[...])
    for i in range(2):

        @pl.when(step == i)
        def _():
            emit(i * unit, unit)

    @pl.when(step == 1)
    def _():
        width = branch_ref.shape[1]
        total[:, :width] = dot_tn(attn_ref[...], branch_ref[...])
        emit(2 * unit, width)


def wide_grad(place, h_two, attn, back_pre, back_branch):
    rows, height = h_two.shape
    unit = back_pre.shape[1] // 4
    narrow = back_branch.shape[1] // 2
    shape = (2, 2, 4, height // 16, 2 * unit + narrow)
    whole = pl.BlockSpec((rows, height), lambda i, j, place: (0, 0))
    out = pl.BlockSpec((2, 1, *shape[2:]), lambda i, j, place: (0, i ^ place[2], 0, 0, 0))
    return pl.pallas_call(
        wide_grad_kernel,
        grid_spec=pltpu.PrefetchScalarGridSpec(
            num_scalar_prefetch=1,
            grid=(2, 2),
            in_specs=[
                whole,
                whole,
                pl.BlockSpec((rows, unit), lambda i, j, place: (0, 2 * i + j)),
                pl.BlockSpec((rows, narrow), lambda i, j, place: (0, i)),
            ],
            out_specs=[out, out],
            scratch_shapes=[pltpu.VMEM((height, unit), F32)],
        ),
        out_shape=[jax.ShapeDtypeStruct(shape, BF16)] * 2,
        compiler_params=pltpu.CompilerParams(
            vmem_limit_bytes=60 * MIB, dimension_semantics=("arbitrary", "arbitrary")
        ),
        cost_estimate=pl.CostEstimate(
            flops=20 * rows * height * unit, bytes_accessed=10 * height * unit, transcendentals=0
        ),
        name="grad_fc_out",
    )(place, h_two, attn, back_pre, back_branch)


def split_grad(place, left, right, by_rows, name):
    rows, height = left.shape
    if by_rows:
        width = right.shape[1]
        tall = height // 4
        shape = (2, 2, 4, height // 32, width)
        specs = [
            pl.BlockSpec((rows, tall), lambda i, place: (0, i)),
            pl.BlockSpec((rows, width), lambda i, place: (0, 0)),
        ]
        out = pl.BlockSpec((2, 2, 1, *shape[3:]), lambda i, place: (0, 0, i, 0, 0))
        steps, total = 4, (tall, width)
    else:
        if right.ndim == 3:
            parts, part = right.shape[0], right.shape[2] // 2
            width = parts * part
            right_spec = pl.BlockSpec((parts, rows, part), lambda i, place: (0, 0, i))
        else:
            width = right.shape[1] // 2
            right_spec = pl.BlockSpec((rows, width), lambda i, place: (0, i))
        shape = (2, 2, 4, height // 16, width)
        specs = [pl.BlockSpec((rows, height), lambda i, place: (0, 0)), right_spec]
        out = pl.BlockSpec((2, 1, *shape[2:]), lambda i, place: (0, i ^ place[2], 0, 0, 0))
        steps, total = 2, (height, width)
    return pl.pallas_call(
        split_grad_kernel,
        grid_spec=pltpu.PrefetchScalarGridSpec(
            num_scalar_prefetch=1,
            grid=(steps,),
            in_specs=specs,
            out_specs=[out, out],
            scratch_shapes=[pltpu.VMEM(total, F32)],
        ),
        out_shape=[jax.ShapeDtypeStruct(shape, BF16)] * 2,
        compiler_params=params(60),
        cost_estimate=pl.CostEstimate(
            flops=4 * rows * steps * total[0] * total[1], bytes_accessed=2 * steps * total[0] * total[1], transcendentals=0
        ),
        name=name,
    )(place, left, right)


def tn_kernel(left_ref, right_ref, out_ref):
    out_ref[...] = dot_tn(left_ref[...], right_ref[...].reshape(left_ref.shape[0], -1)).astype(out_ref.dtype)


def weight_grad(left, right, by_left, name):
    rows = left.shape[0]
    unit = 768
    if right.ndim == 3:
        steps, right_spec = right.shape[0], pl.BlockSpec((1, rows, unit), lambda i: (i, 0, 0))
        shape = (left.shape[1], right.shape[0] * unit)
    else:
        steps = max(left.shape[1], right.shape[1]) // unit
        right_spec = pl.BlockSpec((rows, unit), lambda i: (0, 0 if by_left else i))
        shape = (left.shape[1], right.shape[1])
    return pl.pallas_call(
        tn_kernel,
        grid=(steps,),
        in_specs=[pl.BlockSpec((rows, unit), lambda i: (0, i if by_left else 0)), right_spec],
        out_specs=pl.BlockSpec((unit, unit), lambda i: (i, 0) if by_left else (0, i)),
        out_shape=jax.ShapeDtypeStruct(shape, BF16),
        compiler_params=params(60),
        cost_estimate=pl.CostEstimate(
            flops=2 * rows * shape[0] * shape[1], bytes_accessed=2 * shape[0] * shape[1], transcendentals=0
        ),
        name=name,
    )(left, right)


def qkv_back_kernel(
    x_ref, table_ref, w_ref, back_ref, resid_ref, qkv_sums_ref, mlp_sums_ref, fc_sums_ref, out_ref, small_ref, sums_ref
):
    @pl.when(pl.program_id(0) == 0)
    def _():
        sums_ref[...] = jnp.zeros_like(sums_ref)

    width = x_ref.shape[1]
    back_h = dot_nt(back_ref[0], w_ref[:, :width])
    back_h = back_h + dot_nt(back_ref[1], w_ref[:, width : 2 * width])
    back_h = back_h + dot_nt(back_ref[2], w_ref[:, 2 * width :])
    hat, scale = normalise(x_ref[...].astype(F32))
    out_ref[...] = (resid_ref[...] + normalise_back(back_h * table_ref[0:1], hat, scale)).astype(BF16)
    sums_ref[0:1] += jnp.sum(back_h * hat, axis=0, keepdims=True)
    sums_ref[1:2] += jnp.sum(back_h, axis=0, keepdims=True)

    @pl.when(pl.program_id(0) == pl.num_programs(0) - 1)
    def _():
        half = width // 2
        rows = [sums_ref[0:1], sums_ref[1:2], qkv_sums_ref[0:1], qkv_sums_ref[1:2]]
        rows += [mlp_sums_ref[i : i + 1] for i in (3, 0, 1, 2)]
        halves = [row[:, i * half : (i + 1) * half] for row in rows for i in range(2)]
        hidden = fc_sums_ref.shape[1]
        halves += [fc_sums_ref[:, i * half : (i + 1) * half] for i in range(hidden // half)]
        for i, value in enumerate(halves):
            small_ref[i // 3 : i // 3 + 1, (i % 3) * half : (i % 3 + 1) * half] = value


def qkv_back(x, table, w, back_qkv, back_resid, qkv_sums, mlp_sums, fc_sums):
    rows, width = x.shape
    tile = pl.BlockSpec((ROWS, width), lambda i: (i, 0))
    small = (8, 3 * width // 2)
    return pl.pallas_call(
        qkv_back_kernel,
        grid=(rows // ROWS,),
        in_specs=[
            tile,
            const_spec(table.shape),
            const_spec(w.shape),
            pl.BlockSpec((3, ROWS, width), lambda i: (0, i, 0)),
            tile,
            const_spec(qkv_sums.shape),
            const_spec(mlp_sums.shape),
            const_spec(fc_sums.shape),
        ],
        out_specs=[tile, pl.BlockSpec(small, lambda i: (0, 0))],
        out_shape=[jax.ShapeDtypeStruct((rows, width), BF16), jax.ShapeDtypeStruct(small, F32)],
        scratch_shapes=[pltpu.VMEM((8, width), F32)],
        compiler_params=params(60),
        cost_estimate=pl.CostEstimate(
            flops=18 * rows * width * width, bytes_accessed=20 * rows * width, transcendentals=rows
        ),
        name="qkv_back",
    )(x, table, w, back_qkv, back_resid, qkv_sums, mlp_sums, fc_sums)


def pack_kernel(*refs):
    *vectors, out_ref = refs
    out_ref[...] = jnp.zeros_like(out_ref)
    width = vectors[0].shape[0]
    rows = []
    for ref in vectors:
        value = ref[...].astype(F32).reshape(1, -1)
        rows += [value[:, i * width : (i + 1) * width] for i in range(value.shape[1] // width)]
    out_ref[: len(rows), :width] = jnp.concatenate(rows, axis=0).astype(BF16)


def table_kernel(place_ref, mine_ref, other_ref, table_ref, fc_ref):
    mine = place_ref[0] + 2 * place_ref[1]
    shards = 2 * mine_ref.shape[0]
    own = table_ref.shape[1] // shards
    stored = [ref[i] for i in range(shards // 2) for ref in (mine_ref, other_ref)]
    lanes = stored[0].shape[1]
    total = jnp.zeros((stored[0].shape[0], table_ref.shape[1]), F32)
    spots = lax.broadcasted_iota(jnp.int32, (lanes, table_ref.shape[1]), 1)
    source = lax.broadcasted_iota(jnp.int32, (lanes, table_ref.shape[1]), 0)
    group = own * 4
    fc_spots = lax.broadcasted_iota(jnp.int32, (lanes, group), 1)
    fc_source = lax.broadcasted_iota(jnp.int32, (lanes, group), 0)
    for other in range(shards):
        value = stored[other]
        shard = mine ^ other
        put = (spots == source + shard * own) & (source < own)
        total = total + dot(value, jnp.where(put, 1.0, 0.0).astype(BF16))
    table_ref[...] = total[:8]
    for other in range(shards):
        shard = mine ^ other
        line = jnp.zeros((1, group), F32)
        for k in range(4):
            put = (fc_spots == fc_source + k * own) & (fc_source < own)
            spread_out = dot(stored[other], jnp.where(put, 1.0, 0.0).astype(BF16))
            line = line + spread_out[8 + k : 9 + k]
        fc_ref[:, pl.ds(pl.multiple_of(shard * group, 128), group)] = line


def pack_small(vectors):
    return pl.pallas_call(
        pack_kernel,
        out_shape=jax.ShapeDtypeStruct((48, PAIR), BF16),
        name="pack_small",
    )(*vectors)


def order_small(place, mine, other, width):
    return pl.pallas_call(
        table_kernel,
        in_specs=[smem_spec()] + [pl.BlockSpec(memory_space=pltpu.VMEM)] * 2,
        out_shape=[jax.ShapeDtypeStruct((8, width), F32), jax.ShapeDtypeStruct((1, 4 * width), F32)],
        name="order_small",
    )(place, mine, other)


def swap(value, axis, bit):
    count = lax.axis_size(axis)
    return lax.ppermute(value, axis, [(i, i ^ bit) for i in range(count)])


EARLY = True
FIRST_PAIRS = 2
CORE, X, Y = ("shard", 1), ("rep", 1), ("rep", 2)


def planes(value):
    return [swap(value, "shard", 2 * k) for k in range(1, 4)]


def own_quarter(value, across, along):
    rows, cols = value.shape
    return lax.dynamic_slice(value, (along * (rows // 2), across * (cols // 2)), (rows // 2, cols // 2))


def both_cores(own, own_other, quarters):
    return [*own, *quarters], [*own_other, *(swap(piece, *CORE) for piece in quarters)]


def after(value, *others):
    return lax.optimization_barrier((value, *others))[0]


def merged(tall, wide):
    rows = wide.shape[-2]
    return jnp.concatenate([tall[..., :rows, :], tall[..., rows:, :], wide], axis=-1)


def add(*terms):
    total = terms[0].astype(F32)
    for term in terms[1:]:
        total = total + term.astype(F32)
    return total


def settle(quarters, across, along):
    first = across == 0
    rows = []
    for a, b in (quarters[:2], quarters[2:]):
        rows.append((jnp.where(first, a, b), jnp.where(first, b, a)))
    first = along == 0
    top = [jnp.where(first, a, b) for a, b in zip(*rows)]
    bottom = [jnp.where(first, b, a) for a, b in zip(*rows)]
    return top, bottom


def blocks_of(top, bottom, axis=1):
    return jnp.concatenate([jnp.concatenate(top, axis=axis), jnp.concatenate(bottom, axis=axis)], axis=0).astype(F32)


def gather(value):
    return lax.all_gather(value, "shard", axis=0, tiled=True)


def spread(value):
    own = lax.psum_scatter(value.astype(BF16), "shard", scatter_dimension=0, tiled=True)
    return lax.psum(own, "rep").astype(F32)


def small_tables(rows, width):
    shards = rows.shape[0]
    own = width // shards
    table = rows[:, : 8 * own].reshape(shards, 8, own).transpose(1, 0, 2).reshape(8, width)
    return table, rows[:, 8 * own :].reshape(1, -1)


def small_row(ln1_gain, ln1_bias, q_bias, v_bias, out_bias, ln2_gain, ln2_bias, proj_bias, fc_bias):
    return jnp.concatenate(
        [ln1_gain, ln1_bias, q_bias, v_bias, out_bias, ln2_gain, ln2_bias, proj_bias, fc_bias]
    ).reshape(1, -1)


def local(
    tokens,
    cotangent,
    seq_lengths,
    seq_blocks,
    ln1_gain,
    ln1_bias,
    w_qkv,
    q_bias,
    v_bias,
    w_out,
    out_bias,
    ln2_gain,
    ln2_bias,
    w_fc,
    fc_bias,
    w_proj,
    proj_bias,
):
    width = tokens.shape[1]
    shards = lax.axis_size("shard")
    own = w_qkv.shape[0]
    cut = lax.axis_size("rep") == 4 and shards == 8
    mine, copy = lax.axis_index("shard"), lax.axis_index("rep")
    across, along = copy & 1, copy >> 1
    place = jnp.stack([mine & 1, mine >> 1, across, along]).astype(jnp.int32)
    vectors = (ln1_gain, ln1_bias, q_bias, v_bias, out_bias, ln2_gain, ln2_bias, proj_bias, fc_bias)
    sequences = (seq_lengths, seq_blocks)
    pairs = width // PAIR

    same_core = [[core + 2 * k for k in range(shards // 2)] for core in range(2)]

    def level(value):
        return lax.all_gather(value, "shard", axis=0)

    def foreign(value):
        return jnp.stack([lax.dynamic_index_in_dim(value, mine ^ (2 * k), 0, False) for k in range(1, 4)])

    if cut:
        small = pack_small(vectors)
        part = jnp.concatenate([own_quarter(w_qkv, across, along), small], axis=1)
        others = planes(part)
        columns = part.shape[1] - PAIR
        tall = w_proj.shape[0] // 4
        part_p = lax.dynamic_slice(w_proj, ((2 * along + across) * tall, 0), (tall, width))
        part_w = jnp.concatenate([own_quarter(w_fc, across, along), own_quarter(w_out, across, along)], axis=1)

        small_mine = jnp.stack([small[:16]] + [block[:16, columns:] for block in others])
        small_other = swap(small_mine, *CORE)
        table, fc_shift = order_small(place, small_mine, small_other, width)
        relay = jnp.stack([block[:, :columns] for block in others])
        quarters = [relay, swap(relay, *X), swap(relay, *Y), swap(relay, "rep", 3)]
        own_other = [swap(value, *CORE) for value in (w_qkv, w_fc, w_out, w_proj)]
        mine_pieces, other_pieces = both_cores([w_qkv], own_other[:1], quarters)
        level_w, level_p = level(after(part_w, part)), level(after(part_p, part))
        relay_w = foreign(after(level_w, relay))
        quarters_w = [relay_w, swap(relay_w, *X), swap(relay_w, *Y), swap(relay_w, "rep", 3)]
        x_in = after(tokens, relay_w, own_other) if EARLY else tokens
        h_one, qkv, full_qkv = project_qkv(place, x_in, table, mine_pieces + other_pieces)
        begun = attend(*sequences, qkv, 0, FIRST_PAIRS)
        quarters_w = after(quarters_w, begun)
        mine_w, other_w = both_cores([w_fc, w_out], own_other[1:3], quarters_w)
        relay_p = foreign(after(level_p, begun, quarters_w))
        quarters_p = [relay_p, swap(relay_p, *X), swap(relay_p, *Y), swap(relay_p, "rep", 3)]
        attn, logs = attend(*sequences, qkv, FIRST_PAIRS, pairs - FIRST_PAIRS, after(begun, relay_p, other_w))
        quarters_p = after(quarters_p, attn)
        mine_p, other_p = both_cores([w_proj], own_other[3:], quarters_p)
        mlp_pieces = mine_w + other_w + mine_p + other_p
    else:
        small_all = gather(small_row(*vectors)).astype(F32)
        table, fc_shift = small_tables(small_all, width)
        mlp_pieces = [gather(w_out), gather(w_fc), gather(w_proj)]
        h_one, qkv, full_qkv = project_qkv(place, tokens, table, [gather(w_qkv)])
        attn, logs = attend(*sequences, qkv, 0, pairs)
    output, h_two, act, back_mlp, back_pre, back_resid, back_branch, back_attn, mlp_sums, fc_sums = mlp_both_ways(
        place, *sequences, tokens, attn, cotangent, table, fc_shift, mlp_pieces
    )
    half = width // 2

    if not cut:
        grad_proj = spread(weight_grad(act, back_mlp, True, "grad_proj"))
        grad_fc = spread(weight_grad(h_two, back_pre, False, "grad_fc"))
        grad_out = spread(weight_grad(attn, back_branch, False, "grad_out"))
        back_qkv, qkv_sums = attend_back(*sequences, qkv, attn, back_attn, logs, 0, pairs)
        grad_qkv = spread(weight_grad(h_one, back_qkv, False, "grad_qkv"))
        token_grad, small = qkv_back(tokens, table, full_qkv, back_qkv, back_resid, qkv_sums, mlp_sums, fc_sums)
        small = small.reshape(-1)
        one = [spread(small[i * width : (i + 1) * width]) for i in range(8)]
        fc_row = spread(small[8 * width :])
    else:
        keep_w, send_w = wide_grad(place, h_two, attn, back_pre, back_branch)
        got_w = swap(send_w, *CORE)
        keep_p, send_p = split_grad(place, act, after(back_mlp, send_w), True, "grad_proj")
        got_p = swap(send_p, *CORE)
        got_w = after(got_w, send_p)
        out_w = add(keep_w[1], got_w[1]).astype(BF16)
        far_w = swap(out_w, *Y)
        out_p = add(keep_p[:, 1], got_p[:, 1]).astype(BF16)
        near_p = swap(out_p, *X)
        most = pairs - 1
        early = attend_back(*sequences, qkv, attn, after(back_attn, out_p, out_w), logs, 0, most)
        near_p, far_w = after((near_p, far_w), early)
        out_p = add(keep_p[1, 0], got_p[1, 0], near_p[1]).astype(BF16)
        far_p = swap(out_p, *Y)
        out_w = add(keep_w[0, 1], got_w[0, 1], far_w[1]).astype(BF16)
        near_w = swap(out_w, *X)
        back_qkv, qkv_sums = attend_back(
            *sequences, qkv, attn, back_attn, logs, most, pairs - most, after(early, out_p, out_w)
        )
        keep_q, send_q = split_grad(place, h_one, back_qkv, False, "grad_qkv")
        got_q = swap(send_q, *CORE)
        far_p, near_w = after((far_p, near_w), send_q)
        sum_g = merged(
            add(keep_p[0, 0], got_p[0, 0], near_p[0], far_p), add(keep_w[0, 0], got_w[0, 0], far_w[0], near_w)
        )
        outs_g = sum_g.astype(BF16)
        own_g = lax.psum_scatter(outs_g, "shard", scatter_dimension=0, axis_index_groups=same_core)

        def summed(y, x):
            return add(keep_q[y, x], got_q[y, x])

        keep_q, got_q = after((keep_q, got_q), outs_g)
        outs_q = [summed(0, 1).astype(BF16), summed(1, 0).astype(BF16), summed(1, 1).astype(BF16)]
        parts = [swap(out, "rep", k) for k, out in enumerate(outs_q, 1)]
        token_grad, small = qkv_back(
            tokens, table, full_qkv, back_qkv, after(back_resid, outs_g, outs_q), qkv_sums, mlp_sums, fc_sums
        )
        small = add(small, swap(small, *CORE))
        parts = after(parts, small)

        sum_q = summed(0, 0) + add(*parts)
        outs_q = [jnp.concatenate([sum_q[k], small], axis=0).astype(BF16) for k in range(4)]
        planes_q = [swap(outs_q[k], "shard", 2 * k) for k in range(1, 4)]
        own_g = after(own_g, outs_q)
        all_g = [own_g, swap(own_g, *X), swap(own_g, *Y), swap(own_g, "rep", 3)]
        high = own // 2
        half = w_fc.shape[1] // 2
        cuts = [0, width, 2 * width, 2 * width + half, own_g.shape[1]]
        settled = [
            settle([value[:, cuts[i] : cuts[i + 1]] for value in all_g], across, along) for i in range(4)
        ]
        (first_top, first_bottom), (second_top, second_bottom) = settled[:2]
        grad_proj = jnp.concatenate(
            [
                block
                for one, two in ((first_top, second_top), (first_bottom, second_bottom))
                for i in range(2)
                for block in (one[i], two[i])
            ],
            axis=0,
        ).astype(F32)
        grad_fc, grad_out = blocks_of(*settled[2]), blocks_of(*settled[3])

        own_q = add(outs_q[0], *planes_q).astype(BF16)
        all_q = [own_q, swap(own_q, *X), swap(own_q, *Y), swap(own_q, "rep", 3)]
        half = width // 2
        top, bottom = settle([value[:high] for value in all_q], across, along)
        grad_qkv = jnp.concatenate(
            [
                blocks_of(*[[piece[:, i * half : (i + 1) * half] for piece in line] for line in (top, bottom)])
                for i in range(3)
            ],
            axis=1,
        )
        small = add(*[value[high:] for value in all_q]).reshape(-1)
        one = [lax.dynamic_slice(small, (i * width + mine * own,), (own,)) for i in range(8)]
        fc_row = lax.dynamic_slice(small, (8 * width + mine * 4 * own,), (4 * own,))
    return (
        output,
        token_grad,
        one[0],
        one[1],
        grad_qkv,
        one[2],
        one[3],
        grad_out,
        one[4],
        one[5],
        one[6],
        grad_fc,
        fc_row,
        grad_proj,
        one[7],
    )


def solution(mesh):
    both = ("rep", "shard")
    matrix, vector = P("shard", None), P("shard")
    return jax.shard_map(
        local,
        mesh=mesh,
        in_specs=(
            P(both, None),
            P(both, None),
            P(both),
            P(both),
            vector,
            vector,
            matrix,
            vector,
            vector,
            matrix,
            vector,
            vector,
            vector,
            matrix,
            vector,
            matrix,
            vector,
        ),
        out_specs=(
            P(both, None),
            P(both, None),
            vector,
            vector,
            matrix,
            vector,
            vector,
            matrix,
            vector,
            vector,
            vector,
            matrix,
            vector,
            matrix,
            vector,
        ),
        check_vma=False,
    )
```

```python
import functools

import jax
import jax.numpy as jnp
from jax import lax
from jax.experimental import pallas as pl
from jax.experimental.pallas import tpu as pltpu
from jax.sharding import PartitionSpec as P

HEADS = 12
HEAD_DIM = 64
BLOCK = 128
PAIR = 2 * HEAD_DIM
ROWS = 256
MASKED = -1e30
MIB = 1 << 20
F32 = jnp.float32
BF16 = jnp.bfloat16


def dot(left, right):
    return lax.dot_general(left, right, (((1,), (0,)), ((), ())), preferred_element_type=F32)


def dot_nt(left, right):
    return lax.dot_general(left, right, (((1,), (1,)), ((), ())), preferred_element_type=F32)


def dot_tn(left, right):
    return lax.dot_general(left, right, (((0,), (0,)), ((), ())), preferred_element_type=F32)


def normalise(values):
    average = jnp.mean(values, axis=-1, keepdims=True)
    centred = values - average
    variance = jnp.mean(centred * centred, axis=-1, keepdims=True)
    scale = lax.rsqrt(variance + 1e-05)
    return centred * scale, scale


def normalise_back(back_hat, hat, scale):
    inner = jnp.mean(back_hat * hat, axis=-1, keepdims=True)
    return scale * (back_hat - jnp.mean(back_hat, axis=-1, keepdims=True) - hat * inner)


def live_rows(lengths_ref, blocks_ref, first_row, shape):
    rows = first_row + lax.broadcasted_iota(jnp.int32, shape, 0)
    live = None
    for slot in range(lengths_ref.shape[0]):
        start = blocks_ref[slot] * BLOCK
        inside = (rows >= start) & (rows < start + lengths_ref[slot])
        live = inside if live is None else live | inside
    return live


def const_spec(shape):
    return pl.BlockSpec(shape, lambda *_: (0,) * len(shape), pipeline_mode=pl.Buffered(1))


def smem_spec():
    return pl.BlockSpec(memory_space=pltpu.SMEM)


def params(mib):
    return pltpu.CompilerParams(vmem_limit_bytes=mib * MIB, dimension_semantics=("arbitrary",))


def piece_copies(place_ref, target, pieces, sems, by_rows, first_col=0):
    core, plane, across, along = (place_ref[i] for i in range(4))
    shard_rows, cols = pieces[0][0].shape
    if by_rows:
        rows, half = shard_rows // 4, cols
    else:
        rows, half = shard_rows // 2, cols // 2
    copies = []

    def add(source, row, col):
        sem = sems.at[len(copies)]
        copies.append(pltpu.make_async_copy(source, target.at[pl.ds(row, source.shape[0]), col], sem))

    for other_core in range(2):
        own, *quarters = pieces[other_core]
        add(own, pl.multiple_of((plane * 2 + (core ^ other_core)) * shard_rows, 16), slice(None))
        for other_plane in range(1, 4):
            base = ((plane ^ other_plane) * 2 + (core ^ other_core)) * shard_rows
            for quarter in range(4):
                low, high = across ^ (quarter & 1), along ^ (quarter >> 1)
                block = quarters[quarter].at[other_plane - 1]
                if by_rows:
                    add(block, pl.multiple_of(base + (2 * high + low) * rows, 16), slice(None))
                else:
                    source = block.at[:, pl.ds(first_col, half)]
                    column = pl.ds(pl.multiple_of(low * half, 128), half)
                    add(source, pl.multiple_of(base + high * rows, 16), column)
    return copies


PIECES = 10
COPIES = 26


def any_spec():
    return pl.BlockSpec(memory_space=pl.ANY)


def split_pieces(refs):
    return [refs[: PIECES // 2], refs[PIECES // 2 :]]


def qkv_kernel(place_ref, x_ref, table_ref, *refs):
    *pieces, h_ref, qkv_ref, w_ref, sems = refs
    copies = []
    if len(pieces) == PIECES:
        copies = piece_copies(place_ref, w_ref, split_pieces(pieces), sems, False)
    else:
        copies = [pltpu.make_async_copy(pieces[0], w_ref, sems.at[0])]
    first = pl.program_id(0) == 0

    @pl.when(first)
    def _():
        for copy in copies:
            copy.start()

    hat, _ = normalise(x_ref[...].astype(F32))
    h_one = (hat * table_ref[0:1] + table_ref[1:2]).astype(BF16)
    h_ref[...] = h_one
    width = x_ref.shape[1]

    @pl.when(first)
    def _():
        for copy in copies:
            copy.wait()

    for part in range(3):
        cols = slice(part * width, (part + 1) * width)
        out = dot(h_one, w_ref[:, cols])
        if part != 1:
            out = out + table_ref[2 + part // 2 : 3 + part // 2]
        out = out.astype(BF16)
        if part == 0:
            out = out * BF16(HEAD_DIM**-0.5)
        qkv_ref[:, cols] = out


def project_qkv(place, x, table, pieces):
    rows, width = x.shape
    wide = 3 * width
    return pl.pallas_call(
        qkv_kernel,
        grid=(rows // ROWS,),
        in_specs=[
            smem_spec(),
            pl.BlockSpec((ROWS, width), lambda i: (i, 0)),
            const_spec(table.shape),
        ]
        + [any_spec()] * len(pieces),
        out_specs=[
            pl.BlockSpec((ROWS, width), lambda i: (i, 0)),
            pl.BlockSpec((ROWS, wide), lambda i: (i, 0)),
            const_spec((width, wide)),
        ],
        out_shape=[
            jax.ShapeDtypeStruct((rows, width), BF16),
            jax.ShapeDtypeStruct((rows, wide), BF16),
            jax.ShapeDtypeStruct((width, wide), BF16),
        ],
        scratch_shapes=[pltpu.SemaphoreType.DMA((COPIES,))],
        compiler_params=params(60),
        cost_estimate=pl.CostEstimate(
            flops=6 * rows * width * wide, bytes_accessed=2 * width * wide + 10 * rows * width, transcendentals=rows
        ),
        name="ln1_qkv",
    )(place, x, table, *pieces)


def segment_lanes(lengths_ref, blocks_ref, penalty_ref, member_ref):
    rows = penalty_ref.shape[0]
    shape = (rows, PAIR)
    first = lax.broadcasted_iota(jnp.int32, shape, 0) & ~(BLOCK - 1)
    lane = lax.broadcasted_iota(jnp.int32, shape, 1) & (HEAD_DIM - 1)
    slots = lengths_ref.shape[0]
    member = jnp.full(shape, slots, jnp.int32)
    for slot in range(slots):
        start = blocks_ref[slot] * BLOCK
        inside = (first >= start) & (first < start + lengths_ref[slot])
        member = jnp.where(inside, slot, member)
    same = member == lane
    member_ref[...] = jnp.where(same, 1.0, 0.0).astype(BF16)
    penalty_ref[...] = jnp.where(same | (lane > slots), 0.0, MASKED).astype(BF16)


def low_lanes(rows):
    return lax.broadcasted_iota(jnp.int32, (rows, PAIR), 1) < HEAD_DIM


def attend_kernel(
    lengths_ref, blocks_ref, q_ref, k_ref, v_ref, *refs
):
    out_ref, log_ref, penalty_ref, member_ref, key_ref, value_ref = refs[-6:]
    rows = q_ref.shape[0]

    @pl.when(pl.program_id(0) == 0)
    def _():
        segment_lanes(lengths_ref, blocks_ref, penalty_ref, member_ref)

    low = low_lanes(rows)
    one = jnp.ones((), BF16)
    key_ref[0] = jnp.where(low, k_ref[...], member_ref[...])
    key_ref[1] = jnp.where(low, member_ref[...], k_ref[...])
    value_ref[0] = jnp.where(low, v_ref[...], one)
    value_ref[1] = jnp.where(low, one, v_ref[...])
    low = low_lanes(ROWS)
    causal = lax.broadcasted_iota(jnp.int32, (ROWS, ROWS), 1) <= lax.broadcasted_iota(jnp.int32, (ROWS, ROWS), 0)
    big = 4 * ROWS

    def enter(block, head):
        base = block * big
        q, penalty = q_ref[base : base + big], penalty_ref[base : base + big]
        wide_low = low_lanes(big)
        q_head = jnp.where(wide_low, q, penalty) if head == 0 else jnp.where(wide_low, penalty, q)
        far = dot_nt(q_head, key_ref[head, :base]) if block else None
        pieces = []
        for part in range(4):
            rows_here = slice(part * ROWS, (part + 1) * ROWS)
            first = base + part * ROWS
            near = jnp.where(causal, dot_nt(q_head[rows_here], key_ref[head, first : first + ROWS]), MASKED)
            found = [(first, first + ROWS, near)]
            if part:
                found.append((base, first, dot_nt(q_head[rows_here], key_ref[head, base:first])))
            if block:
                found.append((0, base, far[rows_here]))
            pieces.append(found)
        return pieces

    def leave(found, head):
        largest = None
        for _, _, scores in found:
            peak = jnp.max(scores, axis=-1, keepdims=True)
            largest = peak if largest is None else jnp.maximum(largest, peak)
        total = None
        for first, last, scores in found:
            term = dot(jnp.exp(scores - largest).astype(BF16), value_ref[head, first:last])
            total = term if total is None else total + term
        weight = pltpu.roll(total, HEAD_DIM, 1)
        return total / weight, largest + jnp.log(weight)

    units = [(block, head) for block in range(rows // big) for head in range(2)]
    ahead = enter(*units[0])
    for index, (block, head) in enumerate(units):
        pieces = ahead
        if index + 1 < len(units):
            ahead = enter(*units[index + 1])
        done = [leave(found, head) for found in pieces]
        if head == 0:
            kept = done
            continue
        for part in range(4):
            here = slice(block * big + part * ROWS, block * big + (part + 1) * ROWS)
            out = jnp.where(low, kept[part][0], done[part][0]).astype(BF16)
            live = live_rows(lengths_ref, blocks_ref, here.start, (ROWS, PAIR))
            out_ref[here] = jnp.where(live, out, v_ref[here])
            turned = jnp.where(low, kept[part][1], done[part][1]).T
            log_ref[0, 0:1, here] = turned[0:1]
            log_ref[0, 1:2, here] = turned[HEAD_DIM : HEAD_DIM + 1]


def attend(lengths, blocks, qkv, first, count, earlier=()):
    rows = qkv.shape[0]
    width = qkv.shape[1] // 3
    pairs = width // PAIR
    return pl.pallas_call(
        attend_kernel,
        grid=(count,),
        in_specs=[
            smem_spec(),
            smem_spec(),
            pl.BlockSpec((rows, PAIR), lambda i: (0, first + i)),
            pl.BlockSpec((rows, PAIR), lambda i: (0, pairs + first + i)),
            pl.BlockSpec((rows, PAIR), lambda i: (0, 2 * pairs + first + i)),
        ]
        + [any_spec()] * len(earlier),
        out_specs=[
            pl.BlockSpec((rows, PAIR), lambda i: (0, first + i)),
            pl.BlockSpec((1, 2, rows), lambda i: (first + i, 0, 0)),
        ],
        out_shape=[
            jax.ShapeDtypeStruct((rows, width), BF16),
            jax.ShapeDtypeStruct((pairs, 2, rows), F32),
        ],
        scratch_shapes=[
            pltpu.VMEM((rows, PAIR), BF16),
            pltpu.VMEM((rows, PAIR), BF16),
            pltpu.VMEM((2, rows, PAIR), BF16),
            pltpu.VMEM((2, rows, PAIR), BF16),
        ],
        input_output_aliases={5 + i: i for i in range(len(earlier))},
        compiler_params=params(60),
        cost_estimate=pl.CostEstimate(
            flops=27 * rows * rows * count * PAIR,
            bytes_accessed=8 * rows * count * PAIR,
            transcendentals=rows * rows * count,
        ),
        name="attend",
    )(lengths, blocks, qkv, qkv, qkv, *earlier)


def attend_back_kernel(
    lengths_ref,
    blocks_ref,
    q_ref,
    k_ref,
    v_ref,
    out_ref,
    back_ref,
    log_ref,
    *refs,
):
    grad_ref, sums_ref, penalty_ref, member_ref, q_seg, q_own, back_own, q_grad = refs[-8:]
    rows = q_ref.shape[0]

    @pl.when(pl.program_id(0) == 0)
    def _():
        segment_lanes(lengths_ref, blocks_ref, penalty_ref, member_ref)

    low = low_lanes(rows)
    zero = jnp.zeros((), BF16)
    q, back, penalty = q_ref[...], back_ref[...], penalty_ref[...]
    q_seg[0] = jnp.where(low, q, penalty)
    q_seg[1] = jnp.where(low, penalty, q)
    q_own[0] = jnp.where(low, q, zero)
    q_own[1] = jnp.where(low, zero, q)
    back_own[0] = jnp.where(low, back, zero)
    back_own[1] = jnp.where(low, zero, back)
    inner = (back.astype(F32) * out_ref[...].astype(F32)).T
    inner = [jnp.sum(inner[:HEAD_DIM], axis=0, keepdims=True), jnp.sum(inner[HEAD_DIM:], axis=0, keepdims=True)]
    q_grad[...] = jnp.zeros_like(q_grad)
    low = low_lanes(ROWS)
    causal = lax.broadcasted_iota(jnp.int32, (ROWS, ROWS), 0) <= lax.broadcasted_iota(jnp.int32, (ROWS, ROWS), 1)
    value_sum = jnp.zeros((1, PAIR), F32)

    def pick(head, a, b):
        return jnp.where(low, a, b) if head == 0 else jnp.where(low, b, a)

    def enter(block, head, cols):
        here = slice(block * ROWS, (block + 1) * ROWS)
        k_seg, v_own = pick(head, k_ref[here], member_ref[here]), pick(head, v_ref[here], zero)
        return dot_nt(k_seg, q_seg[head, cols]), dot_nt(v_own, back_ref[cols])

    units = []
    for block in range(rows // ROWS):
        spans = [slice(block * ROWS, (block + 1) * ROWS), slice((block + 1) * ROWS, rows)]
        units += [(block, head, cols) for head in range(2) for cols in spans if cols.start < cols.stop]
    ahead = enter(*units[0])
    for index, (block, head, cols) in enumerate(units):
        here = slice(block * ROWS, (block + 1) * ROWS)
        if head == 0 and cols == here:
            key_grad = jnp.zeros((ROWS, PAIR), F32)
            value_grad = jnp.zeros((ROWS, PAIR), F32)
        scores, back_prob = ahead
        if index + 1 < len(units):
            ahead = enter(*units[index + 1])
        prob = jnp.exp(scores - log_ref[0, head : head + 1, cols])
        if cols == here:
            prob = jnp.where(causal, prob, 0.0)
        back_scores = (prob * (back_prob - inner[head][:, cols])).astype(BF16)
        value_grad = value_grad + dot(prob.astype(BF16), back_own[head, cols])
        key_grad = key_grad + dot(back_scores, q_own[head, cols])
        q_grad[:, cols] += dot_tn(pick(head, k_ref[here], zero), back_scores)
        if head == 0 or cols.stop < rows:
            continue
        key_low, value_low = key_grad.astype(BF16), value_grad.astype(BF16)
        grad_ref[1, here] = key_low
        grad_ref[2, here] = value_low
        value_sum = value_sum + jnp.sum(value_low.astype(F32), axis=0, keepdims=True)
    q_low = (q_grad[...].T * (HEAD_DIM**-0.5)).astype(BF16)
    grad_ref[0] = q_low
    sums_ref[0:1] = jnp.sum(q_low.astype(F32), axis=0, keepdims=True)
    sums_ref[1:2] = value_sum


def attend_back(lengths, blocks, qkv, attn, back_attn, logs, first, count, earlier=()):
    rows, width = attn.shape
    pairs = width // PAIR
    own = pl.BlockSpec((rows, PAIR), lambda i: (0, first + i))
    return pl.pallas_call(
        attend_back_kernel,
        grid=(count,),
        in_specs=[
            smem_spec(),
            smem_spec(),
            own,
            pl.BlockSpec((rows, PAIR), lambda i: (0, pairs + first + i)),
            pl.BlockSpec((rows, PAIR), lambda i: (0, 2 * pairs + first + i)),
            own,
            own,
            pl.BlockSpec((1, 2, rows), lambda i: (first + i, 0, 0)),
        ]
        + [any_spec()] * len(earlier),
        out_specs=[
            pl.BlockSpec((3, rows, PAIR), lambda i: (0, 0, first + i)),
            pl.BlockSpec((8, PAIR), lambda i: (0, first + i)),
        ],
        out_shape=[
            jax.ShapeDtypeStruct((3, rows, width), BF16),
            jax.ShapeDtypeStruct((8, width), F32),
        ],
        scratch_shapes=[
            pltpu.VMEM((rows, PAIR), BF16),
            pltpu.VMEM((rows, PAIR), BF16),
            pltpu.VMEM((2, rows, PAIR), BF16),
            pltpu.VMEM((2, rows, PAIR), BF16),
            pltpu.VMEM((2, rows, PAIR), BF16),
            pltpu.VMEM((PAIR, rows), F32),
        ],
        input_output_aliases={8 + i: i for i in range(len(earlier))},
        compiler_params=params(60),
        cost_estimate=pl.CostEstimate(
            flops=37 * rows * rows * count * PAIR,
            bytes_accessed=16 * rows * count * PAIR,
            transcendentals=rows * rows * count,
        ),
        name="attend_back",
    )(lengths, blocks, qkv, qkv, qkv, attn, back_attn, logs, *earlier)


def mlp_kernel(
    place_ref,
    lengths_ref,
    blocks_ref,
    x_ref,
    attn_ref,
    cot_ref,
    table_ref,
    fc_bias_ref,
    *refs,
):
    *pieces, output_ref, h_ref, act_ref, back_mlp_ref, back_pre_ref = refs[:-9]
    back_resid_ref, back_branch_ref, back_attn_ref, sums_ref, fc_sums_ref, w_out_ref, w_fc_ref, w_proj_ref, sems = refs[-9:]
    if len(pieces) == 22:
        wide_pieces = [pieces[:6], pieces[6:12]]
        fc_pieces, out_pieces = ([[core[i], *core[2:]] for core in wide_pieces] for i in range(2))
        out_copies = piece_copies(place_ref, w_out_ref, out_pieces, sems, False, fc_pieces[0][0].shape[1] // 2)
        fc_copies = piece_copies(place_ref, w_fc_ref, fc_pieces, sems.at[pl.ds(COPIES, COPIES)], False)
        proj_copies = piece_copies(
            place_ref, w_proj_ref, split_pieces(pieces[12:]), sems.at[pl.ds(2 * COPIES, COPIES)], True
        )
    else:
        out_copies, fc_copies, proj_copies = (
            [pltpu.make_async_copy(pieces[i], target, sems.at[i])]
            for i, target in enumerate((w_out_ref, w_fc_ref, w_proj_ref))
        )
    first_step = pl.program_id(0) == 0

    @pl.when(first_step)
    def _():
        for copy in out_copies + fc_copies + proj_copies:
            copy.start()
        for copy in out_copies:
            copy.wait()

    step = pl.program_id(0)
    rows, width = x_ref.shape
    hidden = w_fc_ref.shape[1]

    @pl.when(step == 0)
    def _():
        sums_ref[...] = jnp.zeros_like(sums_ref)
        fc_sums_ref[...] = jnp.zeros_like(fc_sums_ref)

    resid = x_ref[...].astype(F32) + dot(attn_ref[...], w_out_ref[...]) + table_ref[4:5]
    hat, scale = normalise(resid)
    gain = table_ref[5:6]
    h_two = (hat * gain + table_ref[6:7]).astype(BF16)
    h_ref[...] = h_two

    @pl.when(first_step)
    def _():
        for copy in fc_copies + proj_copies:
            copy.wait()

    live = live_rows(lengths_ref, blocks_ref, step * rows, (rows, width))
    back_mlp = jnp.where(live, cot_ref[...], jnp.zeros((), BF16))
    back_mlp_ref[...] = back_mlp
    upstream = back_mlp.astype(F32)
    mlp = jnp.zeros((rows, width), F32)
    back_h = jnp.zeros((rows, width), F32)
    starts = list(range(0, hidden, width))

    def enter(first):
        cols = slice(first, first + width)
        return dot(h_two, w_fc_ref[:, cols]) + fc_bias_ref[:, cols], dot_nt(back_mlp, w_proj_ref[cols])

    ahead = enter(starts[0])
    for index, first in enumerate(starts):
        cols = slice(first, first + width)
        pre, back_act = ahead
        if index + 1 < len(starts):
            ahead = enter(starts[index + 1])
        square = pre * pre
        bent = jnp.tanh(pre * (0.7978845608028654 + 0.035677408136300125 * square))
        half = 0.5 * (1.0 + bent)
        act = (pre * half).astype(BF16)
        act_ref[:, cols] = act
        slope = half + 0.5 * pre * (1.0 - bent * bent) * (0.7978845608028654 + 0.1070322242 * square)
        back_pre = (back_act * slope).astype(BF16)
        back_pre_ref[:, cols] = back_pre
        mlp = mlp + dot(act, w_proj_ref[cols])
        back_h = back_h + dot_nt(back_pre, w_fc_ref[:, cols])
        fc_sums_ref[:, cols] += jnp.sum(back_pre.astype(F32), axis=0, keepdims=True)
    output_ref[...] = (resid + mlp + table_ref[7:8]).astype(BF16)
    back_resid = upstream + normalise_back(back_h * gain, hat, scale)
    back_resid_ref[...] = back_resid
    back_branch = back_resid.astype(BF16)
    back_branch_ref[...] = back_branch
    back_attn_ref[...] = dot_nt(back_branch, w_out_ref[...]).astype(BF16)
    sums_ref[0:1] += jnp.sum(back_h * hat, axis=0, keepdims=True)
    sums_ref[1:2] += jnp.sum(back_h, axis=0, keepdims=True)
    sums_ref[2:3] += jnp.sum(upstream, axis=0, keepdims=True)
    sums_ref[3:4] += jnp.sum(back_branch.astype(F32), axis=0, keepdims=True)


def mlp_both_ways(place, lengths, blocks, x, attn, cot, table, fc_bias, pieces):
    rows, width = x.shape
    hidden = fc_bias.shape[1]
    tile = pl.BlockSpec((ROWS, width), lambda i: (i, 0))
    wide = pl.BlockSpec((ROWS, hidden), lambda i: (i, 0))

    def shaped(cols, kind):
        return jax.ShapeDtypeStruct((rows, cols), kind)

    return pl.pallas_call(
        mlp_kernel,
        grid=(rows // ROWS,),
        in_specs=[smem_spec()] * 3
        + [tile, tile, tile, const_spec(table.shape), const_spec((1, hidden))]
        + [any_spec()] * len(pieces),
        out_specs=[tile, tile, wide, tile, wide, tile, tile, tile]
        + [pl.BlockSpec((8, width), lambda i: (0, 0)), pl.BlockSpec((1, hidden), lambda i: (0, 0))],
        out_shape=[
            shaped(width, BF16),
            shaped(width, BF16),
            shaped(hidden, BF16),
            shaped(width, BF16),
            shaped(hidden, BF16),
            shaped(width, F32),
            shaped(width, BF16),
            shaped(width, BF16),
            jax.ShapeDtypeStruct((8, width), F32),
            jax.ShapeDtypeStruct((1, hidden), F32),
        ],
        scratch_shapes=[
            pltpu.VMEM((width, width), BF16),
            pltpu.VMEM((width, hidden), BF16),
            pltpu.VMEM((hidden, width), BF16),
            pltpu.SemaphoreType.DMA((3 * COPIES,)),
        ],
        compiler_params=params(60),
        cost_estimate=pl.CostEstimate(
            flops=8 * rows * width * (width + 2 * hidden),
            bytes_accessed=40 * rows * width,
            transcendentals=rows * hidden,
        ),
        name="mlp",
    )(place, lengths, blocks, x, attn, cot, table, fc_bias, *pieces)


def split_grad_kernel(place_ref, left_ref, right_ref, keep_ref, send_ref, total):
    core, plane, across, along = (place_ref[i] for i in range(4))
    right = right_ref[...]
    if right.ndim == 3:
        right = jnp.concatenate([right[i] for i in range(right.shape[0])], axis=1)
    total[...] = dot_tn(left_ref[...], right)
    rows = keep_ref.shape[3]
    by_rows = keep_ref.shape[2] == 1
    for to, ref in ((core, keep_ref), (1 - core, send_ref)):
        if by_rows:
            for quarter in range(4):
                source = pl.ds(pl.multiple_of((to * 4 + quarter) * rows, 16), rows)
                ref[along ^ (quarter >> 1), across ^ (quarter & 1), 0] = total[source].astype(BF16)
        else:
            for other in range(4):
                for half in range(2):
                    source = pl.ds(pl.multiple_of(((other * 2 + to) * 2 + half) * rows, 16), rows)
                    ref[along ^ half, 0, plane ^ other] = total[source].astype(BF16)


def wide_grad_kernel(place_ref, h_ref, attn_ref, pre_ref, branch_ref, keep_ref, send_ref, total):
    core, plane, _, along = (place_ref[i] for i in range(4))
    step = pl.program_id(1)
    rows, unit = keep_ref.shape[3], pre_ref.shape[1]

    def emit(first, width):
        for to, ref in ((core, keep_ref), (1 - core, send_ref)):
            for other in range(4):
                for half in range(2):
                    source = pl.ds(pl.multiple_of(((other * 2 + to) * 2 + half) * rows, 16), rows)
                    ref[along ^ half, 0, plane ^ other, :, first : first + width] = total[source, :width].astype(BF16)

    total[...] = dot_tn(h_ref[...], pre_ref[...])
    for i in range(2):

        @pl.when(step == i)
        def _():
            emit(i * unit, unit)

    @pl.when(step == 1)
    def _():
        width = branch_ref.shape[1]
        total[:, :width] = dot_tn(attn_ref[...], branch_ref[...])
        emit(2 * unit, width)


def wide_grad(place, h_two, attn, back_pre, back_branch):
    rows, height = h_two.shape
    unit = back_pre.shape[1] // 4
    narrow = back_branch.shape[1] // 2
    shape = (2, 2, 4, height // 16, 2 * unit + narrow)
    whole = pl.BlockSpec((rows, height), lambda i, j, place: (0, 0))
    out = pl.BlockSpec((2, 1, *shape[2:]), lambda i, j, place: (0, i ^ place[2], 0, 0, 0))
    return pl.pallas_call(
        wide_grad_kernel,
        grid_spec=pltpu.PrefetchScalarGridSpec(
            num_scalar_prefetch=1,
            grid=(2, 2),
            in_specs=[
                whole,
                whole,
                pl.BlockSpec((rows, unit), lambda i, j, place: (0, 2 * i + j)),
                pl.BlockSpec((rows, narrow), lambda i, j, place: (0, i)),
            ],
            out_specs=[out, out],
            scratch_shapes=[pltpu.VMEM((height, unit), F32)],
        ),
        out_shape=[jax.ShapeDtypeStruct(shape, BF16)] * 2,
        compiler_params=pltpu.CompilerParams(
            vmem_limit_bytes=60 * MIB, dimension_semantics=("arbitrary", "arbitrary")
        ),
        cost_estimate=pl.CostEstimate(
            flops=20 * rows * height * unit, bytes_accessed=10 * height * unit, transcendentals=0
        ),
        name="grad_fc_out",
    )(place, h_two, attn, back_pre, back_branch)


def split_grad(place, left, right, by_rows, name):
    rows, height = left.shape
    if by_rows:
        width = right.shape[1]
        tall = height // 4
        shape = (2, 2, 4, height // 32, width)
        specs = [
            pl.BlockSpec((rows, tall), lambda i, place: (0, i)),
            pl.BlockSpec((rows, width), lambda i, place: (0, 0)),
        ]
        out = pl.BlockSpec((2, 2, 1, *shape[3:]), lambda i, place: (0, 0, i ^ place[1], 0, 0))
        steps, total = 4, (tall, width)
    else:
        if right.ndim == 3:
            parts, part = right.shape[0], right.shape[2] // 2
            width = parts * part
            right_spec = pl.BlockSpec((parts, rows, part), lambda i, place: (0, 0, i))
        else:
            width = right.shape[1] // 2
            right_spec = pl.BlockSpec((rows, width), lambda i, place: (0, i))
        shape = (2, 2, 4, height // 16, width)
        specs = [pl.BlockSpec((rows, height), lambda i, place: (0, 0)), right_spec]
        out = pl.BlockSpec((2, 1, *shape[2:]), lambda i, place: (0, i ^ place[2], 0, 0, 0))
        steps, total = 2, (height, width)
    return pl.pallas_call(
        split_grad_kernel,
        grid_spec=pltpu.PrefetchScalarGridSpec(
            num_scalar_prefetch=1,
            grid=(steps,),
            in_specs=specs,
            out_specs=[out, out],
            scratch_shapes=[pltpu.VMEM(total, F32)],
        ),
        out_shape=[jax.ShapeDtypeStruct(shape, BF16)] * 2,
        compiler_params=params(60),
        cost_estimate=pl.CostEstimate(
            flops=4 * rows * steps * total[0] * total[1], bytes_accessed=2 * steps * total[0] * total[1], transcendentals=0
        ),
        name=name,
    )(place, left, right)


def tn_kernel(left_ref, right_ref, out_ref):
    out_ref[...] = dot_tn(left_ref[...], right_ref[...].reshape(left_ref.shape[0], -1)).astype(out_ref.dtype)


def weight_grad(left, right, by_left, name):
    rows = left.shape[0]
    unit = 768
    if right.ndim == 3:
        steps, right_spec = right.shape[0], pl.BlockSpec((1, rows, unit), lambda i: (i, 0, 0))
        shape = (left.shape[1], right.shape[0] * unit)
    else:
        steps = max(left.shape[1], right.shape[1]) // unit
        right_spec = pl.BlockSpec((rows, unit), lambda i: (0, 0 if by_left else i))
        shape = (left.shape[1], right.shape[1])
    return pl.pallas_call(
        tn_kernel,
        grid=(steps,),
        in_specs=[pl.BlockSpec((rows, unit), lambda i: (0, i if by_left else 0)), right_spec],
        out_specs=pl.BlockSpec((unit, unit), lambda i: (i, 0) if by_left else (0, i)),
        out_shape=jax.ShapeDtypeStruct(shape, BF16),
        compiler_params=params(60),
        cost_estimate=pl.CostEstimate(
            flops=2 * rows * shape[0] * shape[1], bytes_accessed=2 * shape[0] * shape[1], transcendentals=0
        ),
        name=name,
    )(left, right)


def qkv_back_kernel(
    x_ref, table_ref, w_ref, back_ref, resid_ref, qkv_sums_ref, mlp_sums_ref, fc_sums_ref, out_ref, small_ref, sums_ref
):
    @pl.when(pl.program_id(0) == 0)
    def _():
        sums_ref[...] = jnp.zeros_like(sums_ref)

    width = x_ref.shape[1]
    back_h = dot_nt(back_ref[0], w_ref[:, :width])
    back_h = back_h + dot_nt(back_ref[1], w_ref[:, width : 2 * width])
    back_h = back_h + dot_nt(back_ref[2], w_ref[:, 2 * width :])
    hat, scale = normalise(x_ref[...].astype(F32))
    out_ref[...] = (resid_ref[...] + normalise_back(back_h * table_ref[0:1], hat, scale)).astype(BF16)
    sums_ref[0:1] += jnp.sum(back_h * hat, axis=0, keepdims=True)
    sums_ref[1:2] += jnp.sum(back_h, axis=0, keepdims=True)

    @pl.when(pl.program_id(0) == pl.num_programs(0) - 1)
    def _():
        half = width // 2
        rows = [sums_ref[0:1], sums_ref[1:2], qkv_sums_ref[0:1], qkv_sums_ref[1:2]]
        rows += [mlp_sums_ref[i : i + 1] for i in (3, 0, 1, 2)]
        halves = [row[:, i * half : (i + 1) * half] for row in rows for i in range(2)]
        hidden = fc_sums_ref.shape[1]
        halves += [fc_sums_ref[:, i * half : (i + 1) * half] for i in range(hidden // half)]
        for i, value in enumerate(halves):
            small_ref[i // 3 : i // 3 + 1, (i % 3) * half : (i % 3 + 1) * half] = value


def qkv_back(x, table, w, back_qkv, back_resid, qkv_sums, mlp_sums, fc_sums):
    rows, width = x.shape
    tile = pl.BlockSpec((ROWS, width), lambda i: (i, 0))
    small = (8, 3 * width // 2)
    return pl.pallas_call(
        qkv_back_kernel,
        grid=(rows // ROWS,),
        in_specs=[
            tile,
            const_spec(table.shape),
            const_spec(w.shape),
            pl.BlockSpec((3, ROWS, width), lambda i: (0, i, 0)),
            tile,
            const_spec(qkv_sums.shape),
            const_spec(mlp_sums.shape),
            const_spec(fc_sums.shape),
        ],
        out_specs=[tile, pl.BlockSpec(small, lambda i: (0, 0))],
        out_shape=[jax.ShapeDtypeStruct((rows, width), BF16), jax.ShapeDtypeStruct(small, F32)],
        scratch_shapes=[pltpu.VMEM((8, width), F32)],
        compiler_params=params(60),
        cost_estimate=pl.CostEstimate(
            flops=rows * width * width, bytes_accessed=rows * width, transcendentals=rows
        ),
        name="qkv_back",
    )(x, table, w, back_qkv, back_resid, qkv_sums, mlp_sums, fc_sums)


def pack_kernel(*refs):
    *vectors, out_ref = refs
    out_ref[...] = jnp.zeros_like(out_ref)
    width = vectors[0].shape[0]
    rows = []
    for ref in vectors:
        value = ref[...].astype(F32).reshape(1, -1)
        rows += [value[:, i * width : (i + 1) * width] for i in range(value.shape[1] // width)]
    out_ref[: len(rows), :width] = jnp.concatenate(rows, axis=0).astype(BF16)


def table_kernel(place_ref, mine_ref, other_ref, table_ref, fc_ref):
    mine = place_ref[0] + 2 * place_ref[1]
    shards = 2 * mine_ref.shape[0]
    own = table_ref.shape[1] // shards
    stored = [ref[i] for i in range(shards // 2) for ref in (mine_ref, other_ref)]
    lanes = stored[0].shape[1]
    total = jnp.zeros((stored[0].shape[0], table_ref.shape[1]), F32)
    spots = lax.broadcasted_iota(jnp.int32, (lanes, table_ref.shape[1]), 1)
    source = lax.broadcasted_iota(jnp.int32, (lanes, table_ref.shape[1]), 0)
    group = own * 4
    fc_spots = lax.broadcasted_iota(jnp.int32, (lanes, group), 1)
    fc_source = lax.broadcasted_iota(jnp.int32, (lanes, group), 0)
    for other in range(shards):
        value = stored[other]
        shard = mine ^ other
        put = (spots == source + shard * own) & (source < own)
        total = total + dot(value, jnp.where(put, 1.0, 0.0).astype(BF16))
    table_ref[...] = total[:8]
    for other in range(shards):
        shard = mine ^ other
        line = jnp.zeros((1, group), F32)
        for k in range(4):
            put = (fc_spots == fc_source + k * own) & (fc_source < own)
            spread_out = dot(stored[other], jnp.where(put, 1.0, 0.0).astype(BF16))
            line = line + spread_out[8 + k : 9 + k]
        fc_ref[:, pl.ds(pl.multiple_of(shard * group, 128), group)] = line


def pack_small(vectors):
    return pl.pallas_call(
        pack_kernel,
        out_shape=jax.ShapeDtypeStruct((48, PAIR), BF16),
        name="pack_small",
    )(*vectors)


def order_small(place, mine, other, width):
    return pl.pallas_call(
        table_kernel,
        in_specs=[smem_spec()] + [pl.BlockSpec(memory_space=pltpu.VMEM)] * 2,
        out_shape=[jax.ShapeDtypeStruct((8, width), F32), jax.ShapeDtypeStruct((1, 4 * width), F32)],
        name="order_small",
    )(place, mine, other)


def swap(value, axis, bit):
    count = lax.axis_size(axis)
    return lax.ppermute(value, axis, [(i, i ^ bit) for i in range(count)])


EARLY = True
FIRST_PAIRS = 2
CORE, X, Y = ("shard", 1), ("rep", 1), ("rep", 2)


def planes(value):
    return [swap(value, "shard", 2 * k) for k in range(1, 4)]


def own_quarter(value, across, along):
    rows, cols = value.shape
    return lax.dynamic_slice(value, (along * (rows // 2), across * (cols // 2)), (rows // 2, cols // 2))


def both_cores(own, own_other, quarters):
    return [*own, *quarters], [*own_other, *(swap(piece, *CORE) for piece in quarters)]


def after(value, *others):
    return lax.optimization_barrier((value, *others))[0]


def merged(tall, wide):
    rows = wide.shape[-2]
    return jnp.concatenate([tall[..., :rows, :], tall[..., rows:, :], wide], axis=-1)


def add(*terms):
    total = terms[0].astype(F32)
    for term in terms[1:]:
        total = total + term.astype(F32)
    return total


def settle(quarters, across, along):
    first = across == 0
    rows = []
    for a, b in (quarters[:2], quarters[2:]):
        rows.append((jnp.where(first, a, b), jnp.where(first, b, a)))
    first = along == 0
    top = [jnp.where(first, a, b) for a, b in zip(*rows)]
    bottom = [jnp.where(first, b, a) for a, b in zip(*rows)]
    return top, bottom


def blocks_of(top, bottom, axis=1):
    return jnp.concatenate([jnp.concatenate(top, axis=axis), jnp.concatenate(bottom, axis=axis)], axis=0).astype(F32)


def gather(value):
    return lax.all_gather(value, "shard", axis=0, tiled=True)


def spread(value):
    own = lax.psum_scatter(value.astype(BF16), "shard", scatter_dimension=0, tiled=True)
    return lax.psum(own, "rep").astype(F32)


def small_tables(rows, width):
    shards = rows.shape[0]
    own = width // shards
    table = rows[:, : 8 * own].reshape(shards, 8, own).transpose(1, 0, 2).reshape(8, width)
    return table, rows[:, 8 * own :].reshape(1, -1)


def small_row(ln1_gain, ln1_bias, q_bias, v_bias, out_bias, ln2_gain, ln2_bias, proj_bias, fc_bias):
    return jnp.concatenate(
        [ln1_gain, ln1_bias, q_bias, v_bias, out_bias, ln2_gain, ln2_bias, proj_bias, fc_bias]
    ).reshape(1, -1)


def local(
    tokens,
    cotangent,
    seq_lengths,
    seq_blocks,
    ln1_gain,
    ln1_bias,
    w_qkv,
    q_bias,
    v_bias,
    w_out,
    out_bias,
    ln2_gain,
    ln2_bias,
    w_fc,
    fc_bias,
    w_proj,
    proj_bias,
):
    width = tokens.shape[1]
    shards = lax.axis_size("shard")
    own = w_qkv.shape[0]
    cut = lax.axis_size("rep") == 4 and shards == 8
    mine, copy = lax.axis_index("shard"), lax.axis_index("rep")
    across, along = copy & 1, copy >> 1
    place = jnp.stack([mine & 1, mine >> 1, across, along]).astype(jnp.int32)
    vectors = (ln1_gain, ln1_bias, q_bias, v_bias, out_bias, ln2_gain, ln2_bias, proj_bias, fc_bias)
    sequences = (seq_lengths, seq_blocks)
    pairs = width // PAIR

    same_core = [[core + 2 * k for k in range(shards // 2)] for core in range(2)]

    def level(value):
        return lax.all_gather(value, "shard", axis=0)

    def foreign(value):
        return jnp.stack([lax.dynamic_index_in_dim(value, mine ^ (2 * k), 0, False) for k in range(1, 4)])

    if cut:
        small = pack_small(vectors)
        part = jnp.concatenate([own_quarter(w_qkv, across, along), small], axis=1)
        others = planes(part)
        columns = part.shape[1] - PAIR
        tall = w_proj.shape[0] // 4
        part_p = lax.dynamic_slice(w_proj, ((2 * along + across) * tall, 0), (tall, width))
        part_w = jnp.concatenate([own_quarter(w_fc, across, along), own_quarter(w_out, across, along)], axis=1)

        small_mine = jnp.stack([small[:16]] + [block[:16, columns:] for block in others])
        small_other = swap(small_mine, *CORE)
        table, fc_shift = order_small(place, small_mine, small_other, width)
        relay = jnp.stack([block[:, :columns] for block in others])
        quarters = [relay, swap(relay, *X), swap(relay, *Y), swap(relay, "rep", 3)]
        own_other = [swap(value, *CORE) for value in (w_qkv, w_fc, w_out, w_proj)]
        mine_pieces, other_pieces = both_cores([w_qkv], own_other[:1], quarters)
        level_w, level_p = level(after(part_w, part)), level(after(part_p, part))
        relay_w = foreign(after(level_w, relay))
        quarters_w = [relay_w, swap(relay_w, *X), swap(relay_w, *Y), swap(relay_w, "rep", 3)]
        x_in = after(tokens, relay_w, own_other) if EARLY else tokens
        h_one, qkv, full_qkv = project_qkv(place, x_in, table, mine_pieces + other_pieces)
        begun = attend(*sequences, qkv, 0, FIRST_PAIRS)
        quarters_w = after(quarters_w, begun)
        mine_w, other_w = both_cores([w_fc, w_out], own_other[1:3], quarters_w)
        relay_p = foreign(after(level_p, begun, quarters_w))
        quarters_p = [relay_p, swap(relay_p, *X), swap(relay_p, *Y), swap(relay_p, "rep", 3)]
        attn, logs = attend(*sequences, qkv, FIRST_PAIRS, pairs - FIRST_PAIRS, after(begun, relay_p, other_w))
        quarters_p = after(quarters_p, attn)
        mine_p, other_p = both_cores([w_proj], own_other[3:], quarters_p)
        mlp_pieces = mine_w + other_w + mine_p + other_p
    else:
        small_all = gather(small_row(*vectors)).astype(F32)
        table, fc_shift = small_tables(small_all, width)
        mlp_pieces = [gather(w_out), gather(w_fc), gather(w_proj)]
        h_one, qkv, full_qkv = project_qkv(place, tokens, table, [gather(w_qkv)])
        attn, logs = attend(*sequences, qkv, 0, pairs)
    output, h_two, act, back_mlp, back_pre, back_resid, back_branch, back_attn, mlp_sums, fc_sums = mlp_both_ways(
        place, *sequences, tokens, attn, cotangent, table, fc_shift, mlp_pieces
    )
    half = width // 2

    if not cut:
        grad_proj = spread(weight_grad(act, back_mlp, True, "grad_proj"))
        grad_fc = spread(weight_grad(h_two, back_pre, False, "grad_fc"))
        grad_out = spread(weight_grad(attn, back_branch, False, "grad_out"))
        back_qkv, qkv_sums = attend_back(*sequences, qkv, attn, back_attn, logs, 0, pairs)
        grad_qkv = spread(weight_grad(h_one, back_qkv, False, "grad_qkv"))
        token_grad, small = qkv_back(tokens, table, full_qkv, back_qkv, back_resid, qkv_sums, mlp_sums, fc_sums)
        small = small.reshape(-1)
        one = [spread(small[i * width : (i + 1) * width]) for i in range(8)]
        fc_row = spread(small[8 * width :])
    else:
        keep_w, send_w = wide_grad(place, h_two, attn, back_pre, back_branch)
        got_w = swap(send_w, *CORE)
        keep_p, send_p = split_grad(place, act, after(back_mlp, send_w), True, "grad_proj")
        got_p = swap(send_p, *CORE)
        got_w = after(got_w, send_p)
        out_w = add(keep_w[1], got_w[1]).astype(BF16)
        far_w = swap(out_w, *Y)
        got_p = after(got_p, out_w)
        out_p = add(keep_p[:, 1], got_p[:, 1]).astype(BF16)
        near_p = swap(out_p, *X)
        most = pairs - 1
        early = attend_back(*sequences, qkv, attn, after(back_attn, out_p, out_w), logs, 0, most)
        near_p, far_w = after((near_p, far_w), early)
        out_p = add(keep_p[1, 0], got_p[1, 0], near_p[1]).astype(BF16)
        far_p = swap(out_p, *Y)
        out_w = add(keep_w[0, 1], got_w[0, 1], far_w[1]).astype(BF16)
        near_w = swap(out_w, *X)
        back_qkv, qkv_sums = attend_back(
            *sequences, qkv, attn, back_attn, logs, most, pairs - most, after(early, out_p, out_w)
        )
        keep_q, send_q = split_grad(place, h_one, back_qkv, False, "grad_qkv")
        got_q = swap(send_q, *CORE)
        far_p, near_w = after((far_p, near_w), send_q)
        sum_g = merged(
            add(keep_p[0, 0], got_p[0, 0], near_p[0], far_p), add(keep_w[0, 0], got_w[0, 0], far_w[0], near_w)
        )
        outs_g = [sum_g[k].astype(BF16) for k in range(4)]
        planes_g = [swap(outs_g[k], "shard", 2 * k) for k in range(1, 4)]

        got_q = after(got_q, outs_g)
        out_q = add(keep_q[:, 1], got_q[:, 1]).astype(BF16)
        near_q = swap(out_q, *X)
        token_grad, small = qkv_back(
            tokens, table, full_qkv, back_qkv, after(back_resid, outs_g, out_q), qkv_sums, mlp_sums, fc_sums
        )
        near_q = after(near_q, small)
        out_q = add(keep_q[1, 0], got_q[1, 0], near_q[1]).astype(BF16)
        far_q = swap(out_q, *Y)
        planes_g = after(planes_g, out_q)
        own_g = add(outs_g[0], *planes_g).astype(BF16)
        far_g = swap(own_g, *Y)
        far_q = after(far_q, own_g)

        sum_q = add(keep_q[0, 0], got_q[0, 0], near_q[0], far_q)
        outs_q = [jnp.concatenate([sum_q[k], small], axis=0).astype(BF16) for k in range(4)]
        planes_q = [swap(outs_q[k], "shard", 2 * k) for k in range(1, 4)]
        both_g = jnp.stack([own_g, after(far_g, outs_q)])
        near_g = swap(both_g, *X)
        own_q = add(outs_q[0], *after(planes_q, both_g)).astype(BF16)
        all_q = [own_q, swap(own_q, *X), swap(own_q, *Y), swap(own_q, "rep", 3)]
        high = own // 2
        half = width // 2
        small = add(*[value[high:] for value in all_q])
        small = add(small, swap(small, *CORE)).reshape(-1)
        top, bottom = settle([value[:high] for value in all_q], across, along)
        grad_qkv = jnp.concatenate(
            [
                blocks_of(*[[piece[:, i * half : (i + 1) * half] for piece in line] for line in (top, bottom)])
                for i in range(3)
            ],
            axis=1,
        )
        near_g = after(near_g, own_q)
        all_g = [own_g, near_g[0], both_g[1], near_g[1]]
        half = w_fc.shape[1] // 2
        cuts = [0, width, 2 * width, 2 * width + half, own_g.shape[1]]
        settled = [
            settle([value[:, cuts[i] : cuts[i + 1]] for value in all_g], across, along) for i in range(4)
        ]
        (first_top, first_bottom), (second_top, second_bottom) = settled[:2]
        grad_proj = jnp.concatenate(
            [
                block
                for one, two in ((first_top, second_top), (first_bottom, second_bottom))
                for i in range(2)
                for block in (one[i], two[i])
            ],
            axis=0,
        ).astype(F32)
        grad_fc, grad_out = blocks_of(*settled[2]), blocks_of(*settled[3])
        one = [lax.dynamic_slice(small, (i * width + mine * own,), (own,)) for i in range(8)]
        fc_row = lax.dynamic_slice(small, (8 * width + mine * 4 * own,), (4 * own,))
    return (
        output,
        token_grad,
        one[0],
        one[1],
        grad_qkv,
        one[2],
        one[3],
        grad_out,
        one[4],
        one[5],
        one[6],
        grad_fc,
        fc_row,
        grad_proj,
        one[7],
    )


def solution(mesh):
    both = ("rep", "shard")
    matrix, vector = P("shard", None), P("shard")
    return jax.shard_map(
        local,
        mesh=mesh,
        in_specs=(
            P(both, None),
            P(both, None),
            P(both),
            P(both),
            vector,
            vector,
            matrix,
            vector,
            vector,
            matrix,
            vector,
            vector,
            vector,
            matrix,
            vector,
            matrix,
            vector,
        ),
        out_specs=(
            P(both, None),
            P(both, None),
            vector,
            vector,
            matrix,
            vector,
            vector,
            matrix,
            vector,
            vector,
            vector,
            matrix,
            vector,
            matrix,
            vector,
        ),
        check_vma=False,
    )
```

```python
import functools

import jax
import jax.numpy as jnp
from jax import lax
from jax.experimental import pallas as pl
from jax.experimental.pallas import tpu as pltpu
from jax.sharding import PartitionSpec as P

HEADS = 12
HEAD_DIM = 64
BLOCK = 128
PAIR = 2 * HEAD_DIM
ROWS = 256
MASKED = -1e30
MIB = 1 << 20
F32 = jnp.float32
BF16 = jnp.bfloat16


def dot(left, right):
    return lax.dot_general(left, right, (((1,), (0,)), ((), ())), preferred_element_type=F32)


def dot_nt(left, right):
    return lax.dot_general(left, right, (((1,), (1,)), ((), ())), preferred_element_type=F32)


def dot_tn(left, right):
    return lax.dot_general(left, right, (((0,), (0,)), ((), ())), preferred_element_type=F32)


def normalise(values):
    average = jnp.mean(values, axis=-1, keepdims=True)
    centred = values - average
    variance = jnp.mean(centred * centred, axis=-1, keepdims=True)
    scale = lax.rsqrt(variance + 1e-05)
    return centred * scale, scale


def normalise_back(back_hat, hat, scale):
    inner = jnp.mean(back_hat * hat, axis=-1, keepdims=True)
    return scale * (back_hat - jnp.mean(back_hat, axis=-1, keepdims=True) - hat * inner)


def live_rows(lengths_ref, blocks_ref, first_row, shape):
    rows = first_row + lax.broadcasted_iota(jnp.int32, shape, 0)
    live = None
    for slot in range(lengths_ref.shape[0]):
        start = blocks_ref[slot] * BLOCK
        inside = (rows >= start) & (rows < start + lengths_ref[slot])
        live = inside if live is None else live | inside
    return live


def const_spec(shape):
    return pl.BlockSpec(shape, lambda *_: (0,) * len(shape), pipeline_mode=pl.Buffered(1))


def smem_spec():
    return pl.BlockSpec(memory_space=pltpu.SMEM)


def params(mib):
    return pltpu.CompilerParams(vmem_limit_bytes=mib * MIB, dimension_semantics=("arbitrary",))


def piece_copies(place_ref, target, pieces, sems, by_rows, first_col=0):
    core, plane, across, along = (place_ref[i] for i in range(4))
    shard_rows, cols = pieces[0][0].shape
    if by_rows:
        rows, half = shard_rows // 4, cols
    else:
        rows, half = shard_rows // 2, cols // 2
    copies = []

    def add(source, row, col):
        sem = sems.at[len(copies)]
        copies.append(pltpu.make_async_copy(source, target.at[pl.ds(row, source.shape[0]), col], sem))

    for other_core in range(2):
        own, *quarters = pieces[other_core]
        add(own, pl.multiple_of((plane * 2 + (core ^ other_core)) * shard_rows, 16), slice(None))
        for other_plane in range(1, 4):
            base = ((plane ^ other_plane) * 2 + (core ^ other_core)) * shard_rows
            for quarter in range(4):
                low, high = across ^ (quarter & 1), along ^ (quarter >> 1)
                block = quarters[quarter].at[other_plane - 1]
                if by_rows:
                    add(block, pl.multiple_of(base + (2 * high + low) * rows, 16), slice(None))
                else:
                    source = block.at[:, pl.ds(first_col, half)]
                    column = pl.ds(pl.multiple_of(low * half, 128), half)
                    add(source, pl.multiple_of(base + high * rows, 16), column)
    return copies


PIECES = 10
COPIES = 26


def any_spec():
    return pl.BlockSpec(memory_space=pl.ANY)


def split_pieces(refs):
    return [refs[: PIECES // 2], refs[PIECES // 2 :]]


def qkv_kernel(place_ref, x_ref, table_ref, *refs):
    *pieces, h_ref, qkv_ref, w_ref, sems = refs
    copies = []
    if len(pieces) == PIECES:
        copies = piece_copies(place_ref, w_ref, split_pieces(pieces), sems, False)
    else:
        copies = [pltpu.make_async_copy(pieces[0], w_ref, sems.at[0])]
    first = pl.program_id(0) == 0

    @pl.when(first)
    def _():
        for copy in copies:
            copy.start()

    hat, _ = normalise(x_ref[...].astype(F32))
    h_one = (hat * table_ref[0:1] + table_ref[1:2]).astype(BF16)
    h_ref[...] = h_one
    width = x_ref.shape[1]

    @pl.when(first)
    def _():
        for copy in copies:
            copy.wait()

    for part in range(3):
        cols = slice(part * width, (part + 1) * width)
        out = dot(h_one, w_ref[:, cols])
        if part != 1:
            out = out + table_ref[2 + part // 2 : 3 + part // 2]
        out = out.astype(BF16)
        if part == 0:
            out = out * BF16(HEAD_DIM**-0.5)
        qkv_ref[:, cols] = out


def project_qkv(place, x, table, pieces):
    rows, width = x.shape
    wide = 3 * width
    return pl.pallas_call(
        qkv_kernel,
        grid=(rows // ROWS,),
        in_specs=[
            smem_spec(),
            pl.BlockSpec((ROWS, width), lambda i: (i, 0)),
            const_spec(table.shape),
        ]
        + [any_spec()] * len(pieces),
        out_specs=[
            pl.BlockSpec((ROWS, width), lambda i: (i, 0)),
            pl.BlockSpec((ROWS, wide), lambda i: (i, 0)),
            const_spec((width, wide)),
        ],
        out_shape=[
            jax.ShapeDtypeStruct((rows, width), BF16),
            jax.ShapeDtypeStruct((rows, wide), BF16),
            jax.ShapeDtypeStruct((width, wide), BF16),
        ],
        scratch_shapes=[pltpu.SemaphoreType.DMA((COPIES,))],
        compiler_params=params(60),
        cost_estimate=pl.CostEstimate(
            flops=6 * rows * width * wide, bytes_accessed=2 * width * wide + 10 * rows * width, transcendentals=rows
        ),
        name="ln1_qkv",
    )(place, x, table, *pieces)


def segment_lanes(lengths_ref, blocks_ref, penalty_ref, member_ref):
    rows = penalty_ref.shape[0]
    shape = (rows, PAIR)
    first = lax.broadcasted_iota(jnp.int32, shape, 0) & ~(BLOCK - 1)
    lane = lax.broadcasted_iota(jnp.int32, shape, 1) & (HEAD_DIM - 1)
    slots = lengths_ref.shape[0]
    member = jnp.full(shape, slots, jnp.int32)
    for slot in range(slots):
        start = blocks_ref[slot] * BLOCK
        inside = (first >= start) & (first < start + lengths_ref[slot])
        member = jnp.where(inside, slot, member)
    same = member == lane
    member_ref[...] = jnp.where(same, 1.0, 0.0).astype(BF16)
    penalty_ref[...] = jnp.where(same | (lane > slots), 0.0, MASKED).astype(BF16)


def low_lanes(rows):
    return lax.broadcasted_iota(jnp.int32, (rows, PAIR), 1) < HEAD_DIM


def attend_kernel(
    lengths_ref, blocks_ref, q_ref, k_ref, v_ref, *refs
):
    out_ref, log_ref, penalty_ref, member_ref, key_ref, value_ref = refs[-6:]
    rows = q_ref.shape[0]

    @pl.when(pl.program_id(0) == 0)
    def _():
        segment_lanes(lengths_ref, blocks_ref, penalty_ref, member_ref)

    low = low_lanes(rows)
    one = jnp.ones((), BF16)
    key_ref[0] = jnp.where(low, k_ref[...], member_ref[...])
    key_ref[1] = jnp.where(low, member_ref[...], k_ref[...])
    value_ref[0] = jnp.where(low, v_ref[...], one)
    value_ref[1] = jnp.where(low, one, v_ref[...])
    low = low_lanes(ROWS)
    causal = lax.broadcasted_iota(jnp.int32, (ROWS, ROWS), 1) <= lax.broadcasted_iota(jnp.int32, (ROWS, ROWS), 0)
    big = 4 * ROWS

    def enter(block, head):
        base = block * big
        q, penalty = q_ref[base : base + big], penalty_ref[base : base + big]
        wide_low = low_lanes(big)
        q_head = jnp.where(wide_low, q, penalty) if head == 0 else jnp.where(wide_low, penalty, q)
        far = dot_nt(q_head, key_ref[head, :base]) if block else None
        pieces = []
        for part in range(4):
            rows_here = slice(part * ROWS, (part + 1) * ROWS)
            first = base + part * ROWS
            near = jnp.where(causal, dot_nt(q_head[rows_here], key_ref[head, first : first + ROWS]), MASKED)
            found = [(first, first + ROWS, near)]
            if part:
                found.append((base, first, dot_nt(q_head[rows_here], key_ref[head, base:first])))
            if block:
                found.append((0, base, far[rows_here]))
            pieces.append(found)
        return pieces

    def leave(found, head):
        largest = None
        for _, _, scores in found:
            peak = jnp.max(scores, axis=-1, keepdims=True)
            largest = peak if largest is None else jnp.maximum(largest, peak)
        total = None
        for first, last, scores in found:
            term = dot(jnp.exp(scores - largest).astype(BF16), value_ref[head, first:last])
            total = term if total is None else total + term
        weight = pltpu.roll(total, HEAD_DIM, 1)
        return total / weight, largest + jnp.log(weight)

    units = [(block, head) for block in range(rows // big) for head in range(2)]
    ahead = enter(*units[0])
    for index, (block, head) in enumerate(units):
        pieces = ahead
        if index + 1 < len(units):
            ahead = enter(*units[index + 1])
        done = [leave(found, head) for found in pieces]
        if head == 0:
            kept = done
            continue
        for part in range(4):
            here = slice(block * big + part * ROWS, block * big + (part + 1) * ROWS)
            out = jnp.where(low, kept[part][0], done[part][0]).astype(BF16)
            live = live_rows(lengths_ref, blocks_ref, here.start, (ROWS, PAIR))
            out_ref[here] = jnp.where(live, out, v_ref[here])
            turned = jnp.where(low, kept[part][1], done[part][1]).T
            log_ref[0, 0:1, here] = turned[0:1]
            log_ref[0, 1:2, here] = turned[HEAD_DIM : HEAD_DIM + 1]


def attend(lengths, blocks, qkv, first, count, earlier=()):
    rows = qkv.shape[0]
    width = qkv.shape[1] // 3
    pairs = width // PAIR
    return pl.pallas_call(
        attend_kernel,
        grid=(count,),
        in_specs=[
            smem_spec(),
            smem_spec(),
            pl.BlockSpec((rows, PAIR), lambda i: (0, first + i)),
            pl.BlockSpec((rows, PAIR), lambda i: (0, pairs + first + i)),
            pl.BlockSpec((rows, PAIR), lambda i: (0, 2 * pairs + first + i)),
        ]
        + [any_spec()] * len(earlier),
        out_specs=[
            pl.BlockSpec((rows, PAIR), lambda i: (0, first + i)),
            pl.BlockSpec((1, 2, rows), lambda i: (first + i, 0, 0)),
        ],
        out_shape=[
            jax.ShapeDtypeStruct((rows, width), BF16),
            jax.ShapeDtypeStruct((pairs, 2, rows), F32),
        ],
        scratch_shapes=[
            pltpu.VMEM((rows, PAIR), BF16),
            pltpu.VMEM((rows, PAIR), BF16),
            pltpu.VMEM((2, rows, PAIR), BF16),
            pltpu.VMEM((2, rows, PAIR), BF16),
        ],
        input_output_aliases={5 + i: i for i in range(len(earlier))},
        compiler_params=params(60),
        cost_estimate=pl.CostEstimate(
            flops=27 * rows * rows * count * PAIR,
            bytes_accessed=8 * rows * count * PAIR,
            transcendentals=rows * rows * count,
        ),
        name="attend",
    )(lengths, blocks, qkv, qkv, qkv, *earlier)


def attend_back_kernel(
    lengths_ref,
    blocks_ref,
    q_ref,
    k_ref,
    v_ref,
    out_ref,
    back_ref,
    log_ref,
    *refs,
):
    grad_ref, sums_ref, penalty_ref, member_ref, q_seg, q_own, back_own, q_grad = refs[-8:]
    rows = q_ref.shape[0]

    @pl.when(pl.program_id(0) == 0)
    def _():
        segment_lanes(lengths_ref, blocks_ref, penalty_ref, member_ref)

    low = low_lanes(rows)
    zero = jnp.zeros((), BF16)
    q, back, penalty = q_ref[...], back_ref[...], penalty_ref[...]
    q_seg[0] = jnp.where(low, q, penalty)
    q_seg[1] = jnp.where(low, penalty, q)
    q_own[0] = jnp.where(low, q, zero)
    q_own[1] = jnp.where(low, zero, q)
    back_own[0] = jnp.where(low, back, zero)
    back_own[1] = jnp.where(low, zero, back)
    inner = (back.astype(F32) * out_ref[...].astype(F32)).T
    inner = [jnp.sum(inner[:HEAD_DIM], axis=0, keepdims=True), jnp.sum(inner[HEAD_DIM:], axis=0, keepdims=True)]
    q_grad[...] = jnp.zeros_like(q_grad)
    low = low_lanes(ROWS)
    causal = lax.broadcasted_iota(jnp.int32, (ROWS, ROWS), 0) <= lax.broadcasted_iota(jnp.int32, (ROWS, ROWS), 1)
    value_sum = jnp.zeros((1, PAIR), F32)

    def pick(head, a, b):
        return jnp.where(low, a, b) if head == 0 else jnp.where(low, b, a)

    def enter(block, head, cols):
        here = slice(block * ROWS, (block + 1) * ROWS)
        k_seg, v_own = pick(head, k_ref[here], member_ref[here]), pick(head, v_ref[here], zero)
        return dot_nt(k_seg, q_seg[head, cols]), dot_nt(v_own, back_ref[cols])

    units = []
    for block in range(rows // ROWS):
        spans = [slice(block * ROWS, (block + 1) * ROWS), slice((block + 1) * ROWS, rows)]
        units += [(block, head, cols) for head in range(2) for cols in spans if cols.start < cols.stop]
    ahead = enter(*units[0])
    for index, (block, head, cols) in enumerate(units):
        here = slice(block * ROWS, (block + 1) * ROWS)
        if head == 0 and cols == here:
            key_grad = jnp.zeros((ROWS, PAIR), F32)
            value_grad = jnp.zeros((ROWS, PAIR), F32)
        scores, back_prob = ahead
        if index + 1 < len(units):
            ahead = enter(*units[index + 1])
        prob = jnp.exp(scores - log_ref[0, head : head + 1, cols])
        if cols == here:
            prob = jnp.where(causal, prob, 0.0)
        back_scores = (prob * (back_prob - inner[head][:, cols])).astype(BF16)
        value_grad = value_grad + dot(prob.astype(BF16), back_own[head, cols])
        key_grad = key_grad + dot(back_scores, q_own[head, cols])
        q_grad[:, cols] += dot_tn(pick(head, k_ref[here], zero), back_scores)
        if head == 0 or cols.stop < rows:
            continue
        key_low, value_low = key_grad.astype(BF16), value_grad.astype(BF16)
        grad_ref[1, here] = key_low
        grad_ref[2, here] = value_low
        value_sum = value_sum + jnp.sum(value_low.astype(F32), axis=0, keepdims=True)
    q_low = (q_grad[...].T * (HEAD_DIM**-0.5)).astype(BF16)
    grad_ref[0] = q_low
    sums_ref[0:1] = jnp.sum(q_low.astype(F32), axis=0, keepdims=True)
    sums_ref[1:2] = value_sum


def attend_back(lengths, blocks, qkv, attn, back_attn, logs, first, count, earlier=()):
    rows, width = attn.shape
    pairs = width // PAIR
    own = pl.BlockSpec((rows, PAIR), lambda i: (0, first + i))
    return pl.pallas_call(
        attend_back_kernel,
        grid=(count,),
        in_specs=[
            smem_spec(),
            smem_spec(),
            own,
            pl.BlockSpec((rows, PAIR), lambda i: (0, pairs + first + i)),
            pl.BlockSpec((rows, PAIR), lambda i: (0, 2 * pairs + first + i)),
            own,
            own,
            pl.BlockSpec((1, 2, rows), lambda i: (first + i, 0, 0)),
        ]
        + [any_spec()] * len(earlier),
        out_specs=[
            pl.BlockSpec((3, rows, PAIR), lambda i: (0, 0, first + i)),
            pl.BlockSpec((8, PAIR), lambda i: (0, first + i)),
        ],
        out_shape=[
            jax.ShapeDtypeStruct((3, rows, width), BF16),
            jax.ShapeDtypeStruct((8, width), F32),
        ],
        scratch_shapes=[
            pltpu.VMEM((rows, PAIR), BF16),
            pltpu.VMEM((rows, PAIR), BF16),
            pltpu.VMEM((2, rows, PAIR), BF16),
            pltpu.VMEM((2, rows, PAIR), BF16),
            pltpu.VMEM((2, rows, PAIR), BF16),
            pltpu.VMEM((PAIR, rows), F32),
        ],
        input_output_aliases={8 + i: i for i in range(len(earlier))},
        compiler_params=params(60),
        cost_estimate=pl.CostEstimate(
            flops=37 * rows * rows * count * PAIR,
            bytes_accessed=16 * rows * count * PAIR,
            transcendentals=rows * rows * count,
        ),
        name="attend_back",
    )(lengths, blocks, qkv, qkv, qkv, attn, back_attn, logs, *earlier)


def mlp_kernel(
    place_ref,
    lengths_ref,
    blocks_ref,
    x_ref,
    attn_ref,
    cot_ref,
    table_ref,
    fc_bias_ref,
    *refs,
):
    *pieces, output_ref, h_ref, act_ref, back_mlp_ref, back_pre_ref = refs[:-9]
    back_resid_ref, back_branch_ref, back_attn_ref, sums_ref, fc_sums_ref, w_out_ref, w_fc_ref, w_proj_ref, sems = refs[-9:]
    if len(pieces) == 22:
        wide_pieces = [pieces[:6], pieces[6:12]]
        fc_pieces, out_pieces = ([[core[i], *core[2:]] for core in wide_pieces] for i in range(2))
        out_copies = piece_copies(place_ref, w_out_ref, out_pieces, sems, False, fc_pieces[0][0].shape[1] // 2)
        fc_copies = piece_copies(place_ref, w_fc_ref, fc_pieces, sems.at[pl.ds(COPIES, COPIES)], False)
        proj_copies = piece_copies(
            place_ref, w_proj_ref, split_pieces(pieces[12:]), sems.at[pl.ds(2 * COPIES, COPIES)], True
        )
    else:
        out_copies, fc_copies, proj_copies = (
            [pltpu.make_async_copy(pieces[i], target, sems.at[i])]
            for i, target in enumerate((w_out_ref, w_fc_ref, w_proj_ref))
        )
    first_step = pl.program_id(0) == 0

    @pl.when(first_step)
    def _():
        for copy in out_copies + fc_copies + proj_copies:
            copy.start()
        for copy in out_copies:
            copy.wait()

    step = pl.program_id(0)
    rows, width = x_ref.shape
    hidden = w_fc_ref.shape[1]

    @pl.when(step == 0)
    def _():
        sums_ref[...] = jnp.zeros_like(sums_ref)
        fc_sums_ref[...] = jnp.zeros_like(fc_sums_ref)

    resid = x_ref[...].astype(F32) + dot(attn_ref[...], w_out_ref[...]) + table_ref[4:5]
    hat, scale = normalise(resid)
    gain = table_ref[5:6]
    h_two = (hat * gain + table_ref[6:7]).astype(BF16)
    h_ref[...] = h_two

    @pl.when(first_step)
    def _():
        for copy in fc_copies + proj_copies:
            copy.wait()

    live = live_rows(lengths_ref, blocks_ref, step * rows, (rows, width))
    back_mlp = jnp.where(live, cot_ref[...], jnp.zeros((), BF16))
    back_mlp_ref[...] = back_mlp
    upstream = back_mlp.astype(F32)
    mlp = jnp.zeros((rows, width), F32)
    back_h = jnp.zeros((rows, width), F32)
    starts = list(range(0, hidden, width))

    def enter(first):
        cols = slice(first, first + width)
        return dot(h_two, w_fc_ref[:, cols]) + fc_bias_ref[:, cols], dot_nt(back_mlp, w_proj_ref[cols])

    ahead = enter(starts[0])
    for index, first in enumerate(starts):
        cols = slice(first, first + width)
        pre, back_act = ahead
        if index + 1 < len(starts):
            ahead = enter(starts[index + 1])
        square = pre * pre
        bent = jnp.tanh(pre * (0.7978845608028654 + 0.035677408136300125 * square))
        half = 0.5 * (1.0 + bent)
        act = (pre * half).astype(BF16)
        act_ref[:, cols] = act
        slope = half + 0.5 * pre * (1.0 - bent * bent) * (0.7978845608028654 + 0.1070322242 * square)
        back_pre = (back_act * slope).astype(BF16)
        back_pre_ref[:, cols] = back_pre
        mlp = mlp + dot(act, w_proj_ref[cols])
        back_h = back_h + dot_nt(back_pre, w_fc_ref[:, cols])
        fc_sums_ref[:, cols] += jnp.sum(back_pre.astype(F32), axis=0, keepdims=True)
    output_ref[...] = (resid + mlp + table_ref[7:8]).astype(BF16)
    back_resid = upstream + normalise_back(back_h * gain, hat, scale)
    back_resid_ref[...] = back_resid
    back_branch = back_resid.astype(BF16)
    back_branch_ref[...] = back_branch
    back_attn_ref[...] = dot_nt(back_branch, w_out_ref[...]).astype(BF16)
    sums_ref[0:1] += jnp.sum(back_h * hat, axis=0, keepdims=True)
    sums_ref[1:2] += jnp.sum(back_h, axis=0, keepdims=True)
    sums_ref[2:3] += jnp.sum(upstream, axis=0, keepdims=True)
    sums_ref[3:4] += jnp.sum(back_branch.astype(F32), axis=0, keepdims=True)


def mlp_both_ways(place, lengths, blocks, x, attn, cot, table, fc_bias, pieces):
    rows, width = x.shape
    hidden = fc_bias.shape[1]
    tile = pl.BlockSpec((ROWS, width), lambda i: (i, 0))
    wide = pl.BlockSpec((ROWS, hidden), lambda i: (i, 0))

    def shaped(cols, kind):
        return jax.ShapeDtypeStruct((rows, cols), kind)

    return pl.pallas_call(
        mlp_kernel,
        grid=(rows // ROWS,),
        in_specs=[smem_spec()] * 3
        + [tile, tile, tile, const_spec(table.shape), const_spec((1, hidden))]
        + [any_spec()] * len(pieces),
        out_specs=[tile, tile, wide, tile, wide, tile, tile, tile]
        + [pl.BlockSpec((8, width), lambda i: (0, 0)), pl.BlockSpec((1, hidden), lambda i: (0, 0))],
        out_shape=[
            shaped(width, BF16),
            shaped(width, BF16),
            shaped(hidden, BF16),
            shaped(width, BF16),
            shaped(hidden, BF16),
            shaped(width, F32),
            shaped(width, BF16),
            shaped(width, BF16),
            jax.ShapeDtypeStruct((8, width), F32),
            jax.ShapeDtypeStruct((1, hidden), F32),
        ],
        scratch_shapes=[
            pltpu.VMEM((width, width), BF16),
            pltpu.VMEM((width, hidden), BF16),
            pltpu.VMEM((hidden, width), BF16),
            pltpu.SemaphoreType.DMA((3 * COPIES,)),
        ],
        compiler_params=params(60),
        cost_estimate=pl.CostEstimate(
            flops=8 * rows * width * (width + 2 * hidden),
            bytes_accessed=40 * rows * width,
            transcendentals=rows * hidden,
        ),
        name="mlp",
    )(place, lengths, blocks, x, attn, cot, table, fc_bias, *pieces)


def split_grad_kernel(place_ref, left_ref, right_ref, keep_ref, send_ref, total):
    core, plane, across, along = (place_ref[i] for i in range(4))
    right = right_ref[...]
    if right.ndim == 3:
        right = jnp.concatenate([right[i] for i in range(right.shape[0])], axis=1)
    total[...] = dot_tn(left_ref[...], right)
    rows = keep_ref.shape[3]
    by_rows = keep_ref.shape[2] == 1
    for to, ref in ((core, keep_ref), (1 - core, send_ref)):
        if by_rows:
            for quarter in range(4):
                source = pl.ds(pl.multiple_of((to * 4 + quarter) * rows, 16), rows)
                ref[along ^ (quarter >> 1), across ^ (quarter & 1), 0] = total[source].astype(BF16)
        else:
            for other in range(4):
                for half in range(2):
                    source = pl.ds(pl.multiple_of(((other * 2 + to) * 2 + half) * rows, 16), rows)
                    ref[along ^ half, 0, plane ^ other] = total[source].astype(BF16)


def wide_grad_kernel(place_ref, h_ref, attn_ref, pre_ref, branch_ref, keep_ref, send_ref, total):
    core, plane, _, along = (place_ref[i] for i in range(4))
    step = pl.program_id(1)
    rows, unit = keep_ref.shape[3], pre_ref.shape[1]

    def emit(first, width):
        for to, ref in ((core, keep_ref), (1 - core, send_ref)):
            for other in range(4):
                for half in range(2):
                    source = pl.ds(pl.multiple_of(((other * 2 + to) * 2 + half) * rows, 16), rows)
                    ref[along ^ half, 0, plane ^ other, :, first : first + width] = total[source, :width].astype(BF16)

    total[...] = dot_tn(h_ref[...], pre_ref[...])
    for i in range(2):

        @pl.when(step == i)
        def _():
            emit(i * unit, unit)

    @pl.when(step == 1)
    def _():
        width = branch_ref.shape[1]
        total[:, :width] = dot_tn(attn_ref[...], branch_ref[...])
        emit(2 * unit, width)


def wide_grad(place, h_two, attn, back_pre, back_branch):
    rows, height = h_two.shape
    unit = back_pre.shape[1] // 4
    narrow = back_branch.shape[1] // 2
    shape = (2, 2, 4, height // 16, 2 * unit + narrow)
    whole = pl.BlockSpec((rows, height), lambda i, j, place: (0, 0))
    out = pl.BlockSpec((2, 1, *shape[2:]), lambda i, j, place: (0, i ^ place[2], 0, 0, 0))
    return pl.pallas_call(
        wide_grad_kernel,
        grid_spec=pltpu.PrefetchScalarGridSpec(
            num_scalar_prefetch=1,
            grid=(2, 2),
            in_specs=[
                whole,
                whole,
                pl.BlockSpec((rows, unit), lambda i, j, place: (0, 2 * i + j)),
                pl.BlockSpec((rows, narrow), lambda i, j, place: (0, i)),
            ],
            out_specs=[out, out],
            scratch_shapes=[pltpu.VMEM((height, unit), F32)],
        ),
        out_shape=[jax.ShapeDtypeStruct(shape, BF16)] * 2,
        compiler_params=pltpu.CompilerParams(
            vmem_limit_bytes=60 * MIB, dimension_semantics=("arbitrary", "arbitrary")
        ),
        cost_estimate=pl.CostEstimate(
            flops=20 * rows * height * unit, bytes_accessed=10 * height * unit, transcendentals=0
        ),
        name="grad_fc_out",
    )(place, h_two, attn, back_pre, back_branch)


def split_grad(place, left, right, by_rows, name):
    rows, height = left.shape
    if by_rows:
        width = right.shape[1]
        tall = height // 4
        shape = (2, 2, 4, height // 32, width)
        specs = [
            pl.BlockSpec((rows, tall), lambda i, place: (0, i)),
            pl.BlockSpec((rows, width), lambda i, place: (0, 0)),
        ]
        out = pl.BlockSpec((2, 2, 1, *shape[3:]), lambda i, place: (0, 0, i ^ place[1], 0, 0))
        steps, total = 4, (tall, width)
    else:
        if right.ndim == 3:
            parts, part = right.shape[0], right.shape[2] // 2
            width = parts * part
            right_spec = pl.BlockSpec((parts, rows, part), lambda i, place: (0, 0, i))
        else:
            width = right.shape[1] // 2
            right_spec = pl.BlockSpec((rows, width), lambda i, place: (0, i))
        shape = (2, 2, 4, height // 16, width)
        specs = [pl.BlockSpec((rows, height), lambda i, place: (0, 0)), right_spec]
        out = pl.BlockSpec((2, 1, *shape[2:]), lambda i, place: (0, i ^ place[2], 0, 0, 0))
        steps, total = 2, (height, width)
    return pl.pallas_call(
        split_grad_kernel,
        grid_spec=pltpu.PrefetchScalarGridSpec(
            num_scalar_prefetch=1,
            grid=(steps,),
            in_specs=specs,
            out_specs=[out, out],
            scratch_shapes=[pltpu.VMEM(total, F32)],
        ),
        out_shape=[jax.ShapeDtypeStruct(shape, BF16)] * 2,
        compiler_params=params(60),
        cost_estimate=pl.CostEstimate(
            flops=4 * rows * steps * total[0] * total[1], bytes_accessed=2 * steps * total[0] * total[1], transcendentals=0
        ),
        name=name,
    )(place, left, right)


def tn_kernel(left_ref, right_ref, out_ref):
    out_ref[...] = dot_tn(left_ref[...], right_ref[...].reshape(left_ref.shape[0], -1)).astype(out_ref.dtype)


def weight_grad(left, right, by_left, name):
    rows = left.shape[0]
    unit = 768
    if right.ndim == 3:
        steps, right_spec = right.shape[0], pl.BlockSpec((1, rows, unit), lambda i: (i, 0, 0))
        shape = (left.shape[1], right.shape[0] * unit)
    else:
        steps = max(left.shape[1], right.shape[1]) // unit
        right_spec = pl.BlockSpec((rows, unit), lambda i: (0, 0 if by_left else i))
        shape = (left.shape[1], right.shape[1])
    return pl.pallas_call(
        tn_kernel,
        grid=(steps,),
        in_specs=[pl.BlockSpec((rows, unit), lambda i: (0, i if by_left else 0)), right_spec],
        out_specs=pl.BlockSpec((unit, unit), lambda i: (i, 0) if by_left else (0, i)),
        out_shape=jax.ShapeDtypeStruct(shape, BF16),
        compiler_params=params(60),
        cost_estimate=pl.CostEstimate(
            flops=2 * rows * shape[0] * shape[1], bytes_accessed=2 * shape[0] * shape[1], transcendentals=0
        ),
        name=name,
    )(left, right)


def qkv_back_kernel(
    x_ref, table_ref, w_ref, back_ref, resid_ref, qkv_sums_ref, mlp_sums_ref, fc_sums_ref, out_ref, small_ref, sums_ref
):
    @pl.when(pl.program_id(0) == 0)
    def _():
        sums_ref[...] = jnp.zeros_like(sums_ref)

    width = x_ref.shape[1]
    back_h = dot_nt(back_ref[0], w_ref[:, :width])
    back_h = back_h + dot_nt(back_ref[1], w_ref[:, width : 2 * width])
    back_h = back_h + dot_nt(back_ref[2], w_ref[:, 2 * width :])
    hat, scale = normalise(x_ref[...].astype(F32))
    out_ref[...] = (resid_ref[...] + normalise_back(back_h * table_ref[0:1], hat, scale)).astype(BF16)
    sums_ref[0:1] += jnp.sum(back_h * hat, axis=0, keepdims=True)
    sums_ref[1:2] += jnp.sum(back_h, axis=0, keepdims=True)

    @pl.when(pl.program_id(0) == pl.num_programs(0) - 1)
    def _():
        half = width // 2
        rows = [sums_ref[0:1], sums_ref[1:2], qkv_sums_ref[0:1], qkv_sums_ref[1:2]]
        rows += [mlp_sums_ref[i : i + 1] for i in (3, 0, 1, 2)]
        halves = [row[:, i * half : (i + 1) * half] for row in rows for i in range(2)]
        hidden = fc_sums_ref.shape[1]
        halves += [fc_sums_ref[:, i * half : (i + 1) * half] for i in range(hidden // half)]
        for i, value in enumerate(halves):
            small_ref[i // 3 : i // 3 + 1, (i % 3) * half : (i % 3 + 1) * half] = value


def qkv_back(x, table, w, back_qkv, back_resid, qkv_sums, mlp_sums, fc_sums):
    rows, width = x.shape
    tile = pl.BlockSpec((ROWS, width), lambda i: (i, 0))
    small = (8, 3 * width // 2)
    return pl.pallas_call(
        qkv_back_kernel,
        grid=(rows // ROWS,),
        in_specs=[
            tile,
            const_spec(table.shape),
            const_spec(w.shape),
            pl.BlockSpec((3, ROWS, width), lambda i: (0, i, 0)),
            tile,
            const_spec(qkv_sums.shape),
            const_spec(mlp_sums.shape),
            const_spec(fc_sums.shape),
        ],
        out_specs=[tile, pl.BlockSpec(small, lambda i: (0, 0))],
        out_shape=[jax.ShapeDtypeStruct((rows, width), BF16), jax.ShapeDtypeStruct(small, F32)],
        scratch_shapes=[pltpu.VMEM((8, width), F32)],
        compiler_params=params(60),
        cost_estimate=pl.CostEstimate(
            flops=rows * width * width, bytes_accessed=rows * width, transcendentals=rows
        ),
        name="qkv_back",
    )(x, table, w, back_qkv, back_resid, qkv_sums, mlp_sums, fc_sums)


def pack_kernel(*refs):
    *vectors, out_ref = refs
    out_ref[...] = jnp.zeros_like(out_ref)
    width = vectors[0].shape[0]
    rows = []
    for ref in vectors:
        value = ref[...].astype(F32).reshape(1, -1)
        rows += [value[:, i * width : (i + 1) * width] for i in range(value.shape[1] // width)]
    out_ref[: len(rows), :width] = jnp.concatenate(rows, axis=0).astype(BF16)


def table_kernel(place_ref, mine_ref, other_ref, table_ref, fc_ref):
    mine = place_ref[0] + 2 * place_ref[1]
    shards = 2 * mine_ref.shape[0]
    own = table_ref.shape[1] // shards
    stored = [ref[i] for i in range(shards // 2) for ref in (mine_ref, other_ref)]
    lanes = stored[0].shape[1]
    total = jnp.zeros((stored[0].shape[0], table_ref.shape[1]), F32)
    spots = lax.broadcasted_iota(jnp.int32, (lanes, table_ref.shape[1]), 1)
    source = lax.broadcasted_iota(jnp.int32, (lanes, table_ref.shape[1]), 0)
    group = own * 4
    fc_spots = lax.broadcasted_iota(jnp.int32, (lanes, group), 1)
    fc_source = lax.broadcasted_iota(jnp.int32, (lanes, group), 0)
    for other in range(shards):
        value = stored[other]
        shard = mine ^ other
        put = (spots == source + shard * own) & (source < own)
        total = total + dot(value, jnp.where(put, 1.0, 0.0).astype(BF16))
    table_ref[...] = total[:8]
    for other in range(shards):
        shard = mine ^ other
        line = jnp.zeros((1, group), F32)
        for k in range(4):
            put = (fc_spots == fc_source + k * own) & (fc_source < own)
            spread_out = dot(stored[other], jnp.where(put, 1.0, 0.0).astype(BF16))
            line = line + spread_out[8 + k : 9 + k]
        fc_ref[:, pl.ds(pl.multiple_of(shard * group, 128), group)] = line


def pack_small(vectors):
    return pl.pallas_call(
        pack_kernel,
        out_shape=jax.ShapeDtypeStruct((48, PAIR), BF16),
        name="pack_small",
    )(*vectors)


def order_small(place, mine, other, width):
    return pl.pallas_call(
        table_kernel,
        in_specs=[smem_spec()] + [pl.BlockSpec(memory_space=pltpu.VMEM)] * 2,
        out_shape=[jax.ShapeDtypeStruct((8, width), F32), jax.ShapeDtypeStruct((1, 4 * width), F32)],
        name="order_small",
    )(place, mine, other)


def swap(value, axis, bit):
    count = lax.axis_size(axis)
    return lax.ppermute(value, axis, [(i, i ^ bit) for i in range(count)])


EARLY = True
FIRST_PAIRS = 2
CORE, X, Y = ("shard", 1), ("rep", 1), ("rep", 2)


def planes(value):
    return [swap(value, "shard", 2 * k) for k in range(1, 4)]


def own_quarter(value, across, along):
    rows, cols = value.shape
    return lax.dynamic_slice(value, (along * (rows // 2), across * (cols // 2)), (rows // 2, cols // 2))


def both_cores(own, own_other, quarters):
    return [*own, *quarters], [*own_other, *(swap(piece, *CORE) for piece in quarters)]


def after(value, *others):
    return lax.optimization_barrier((value, *others))[0]


def merged(tall, wide):
    rows = wide.shape[-2]
    return jnp.concatenate([tall[..., :rows, :], tall[..., rows:, :], wide], axis=-1)


def add(*terms):
    total = terms[0].astype(F32)
    for term in terms[1:]:
        total = total + term.astype(F32)
    return total


def settle(quarters, across, along):
    first = across == 0
    rows = []
    for a, b in (quarters[:2], quarters[2:]):
        rows.append((jnp.where(first, a, b), jnp.where(first, b, a)))
    first = along == 0
    top = [jnp.where(first, a, b) for a, b in zip(*rows)]
    bottom = [jnp.where(first, b, a) for a, b in zip(*rows)]
    return top, bottom


def blocks_of(top, bottom, axis=1):
    return jnp.concatenate([jnp.concatenate(top, axis=axis), jnp.concatenate(bottom, axis=axis)], axis=0).astype(F32)


def gather(value):
    return lax.all_gather(value, "shard", axis=0, tiled=True)


def spread(value):
    own = lax.psum_scatter(value.astype(BF16), "shard", scatter_dimension=0, tiled=True)
    return lax.psum(own, "rep").astype(F32)


def small_tables(rows, width):
    shards = rows.shape[0]
    own = width // shards
    table = rows[:, : 8 * own].reshape(shards, 8, own).transpose(1, 0, 2).reshape(8, width)
    return table, rows[:, 8 * own :].reshape(1, -1)


def small_row(ln1_gain, ln1_bias, q_bias, v_bias, out_bias, ln2_gain, ln2_bias, proj_bias, fc_bias):
    return jnp.concatenate(
        [ln1_gain, ln1_bias, q_bias, v_bias, out_bias, ln2_gain, ln2_bias, proj_bias, fc_bias]
    ).reshape(1, -1)


def local(
    tokens,
    cotangent,
    seq_lengths,
    seq_blocks,
    ln1_gain,
    ln1_bias,
    w_qkv,
    q_bias,
    v_bias,
    w_out,
    out_bias,
    ln2_gain,
    ln2_bias,
    w_fc,
    fc_bias,
    w_proj,
    proj_bias,
):
    width = tokens.shape[1]
    shards = lax.axis_size("shard")
    own = w_qkv.shape[0]
    cut = lax.axis_size("rep") == 4 and shards == 8
    mine, copy = lax.axis_index("shard"), lax.axis_index("rep")
    across, along = copy & 1, copy >> 1
    place = jnp.stack([mine & 1, mine >> 1, across, along]).astype(jnp.int32)
    vectors = (ln1_gain, ln1_bias, q_bias, v_bias, out_bias, ln2_gain, ln2_bias, proj_bias, fc_bias)
    sequences = (seq_lengths, seq_blocks)
    pairs = width // PAIR

    same_core = [[core + 2 * k for k in range(shards // 2)] for core in range(2)]

    def level(value):
        return lax.all_gather(value, "shard", axis=0)

    def foreign(value):
        return jnp.stack([lax.dynamic_index_in_dim(value, mine ^ (2 * k), 0, False) for k in range(1, 4)])

    if cut:
        small = pack_small(vectors)
        part = jnp.concatenate([own_quarter(w_qkv, across, along), small], axis=1)
        others = planes(part)
        columns = part.shape[1] - PAIR
        tall = w_proj.shape[0] // 4
        part_p = lax.dynamic_slice(w_proj, ((2 * along + across) * tall, 0), (tall, width))
        part_w = jnp.concatenate([own_quarter(w_fc, across, along), own_quarter(w_out, across, along)], axis=1)

        small_mine = jnp.stack([small[:16]] + [block[:16, columns:] for block in others])
        small_other = swap(small_mine, *CORE)
        table, fc_shift = order_small(place, small_mine, small_other, width)
        relay = jnp.stack([block[:, :columns] for block in others])
        quarters = [relay, swap(relay, *X), swap(relay, *Y), swap(relay, "rep", 3)]
        own_other = [swap(value, *CORE) for value in (w_qkv, w_fc, w_out, w_proj)]
        mine_pieces, other_pieces = both_cores([w_qkv], own_other[:1], quarters)
        level_w, level_p = level(after(part_w, part)), level(after(part_p, part))
        relay_w = foreign(after(level_w, relay))
        quarters_w = [relay_w, swap(relay_w, *X), swap(relay_w, *Y), swap(relay_w, "rep", 3)]
        x_in = after(tokens, relay_w, own_other) if EARLY else tokens
        h_one, qkv, full_qkv = project_qkv(place, x_in, table, mine_pieces + other_pieces)
        begun = attend(*sequences, qkv, 0, FIRST_PAIRS)
        quarters_w = after(quarters_w, begun)
        mine_w, other_w = both_cores([w_fc, w_out], own_other[1:3], quarters_w)
        relay_p = foreign(after(level_p, begun, quarters_w))
        quarters_p = [relay_p, swap(relay_p, *X), swap(relay_p, *Y), swap(relay_p, "rep", 3)]
        attn, logs = attend(*sequences, qkv, FIRST_PAIRS, pairs - FIRST_PAIRS, after(begun, relay_p, other_w))
        quarters_p = after(quarters_p, attn)
        mine_p, other_p = both_cores([w_proj], own_other[3:], quarters_p)
        mlp_pieces = mine_w + other_w + mine_p + other_p
    else:
        small_all = gather(small_row(*vectors)).astype(F32)
        table, fc_shift = small_tables(small_all, width)
        mlp_pieces = [gather(w_out), gather(w_fc), gather(w_proj)]
        h_one, qkv, full_qkv = project_qkv(place, tokens, table, [gather(w_qkv)])
        attn, logs = attend(*sequences, qkv, 0, pairs)
    output, h_two, act, back_mlp, back_pre, back_resid, back_branch, back_attn, mlp_sums, fc_sums = mlp_both_ways(
        place, *sequences, tokens, attn, cotangent, table, fc_shift, mlp_pieces
    )
    half = width // 2

    if not cut:
        grad_proj = spread(weight_grad(act, back_mlp, True, "grad_proj"))
        grad_fc = spread(weight_grad(h_two, back_pre, False, "grad_fc"))
        grad_out = spread(weight_grad(attn, back_branch, False, "grad_out"))
        back_qkv, qkv_sums = attend_back(*sequences, qkv, attn, back_attn, logs, 0, pairs)
        grad_qkv = spread(weight_grad(h_one, back_qkv, False, "grad_qkv"))
        token_grad, small = qkv_back(tokens, table, full_qkv, back_qkv, back_resid, qkv_sums, mlp_sums, fc_sums)
        small = small.reshape(-1)
        one = [spread(small[i * width : (i + 1) * width]) for i in range(8)]
        fc_row = spread(small[8 * width :])
    else:
        keep_w, send_w = wide_grad(place, h_two, attn, back_pre, back_branch)
        got_w = swap(send_w, *CORE)
        keep_p, send_p = split_grad(place, act, after(back_mlp, send_w), True, "grad_proj")
        got_p = swap(send_p, *CORE)
        got_w = after(got_w, send_p)
        out_w = add(keep_w[1], got_w[1]).astype(BF16)
        far_w = swap(out_w, *Y)
        got_p = after(got_p, out_w)
        out_p = add(keep_p[:, 1], got_p[:, 1]).astype(BF16)
        near_p = swap(out_p, *X)
        most = pairs - 1
        early = attend_back(*sequences, qkv, attn, after(back_attn, out_p, out_w), logs, 0, most)
        near_p, far_w = after((near_p, far_w), early)
        out_p = add(keep_p[1, 0], got_p[1, 0], near_p[1]).astype(BF16)
        far_p = swap(out_p, *Y)
        out_w = add(keep_w[0, 1], got_w[0, 1], far_w[1]).astype(BF16)
        near_w = swap(out_w, *X)
        back_qkv, qkv_sums = attend_back(
            *sequences, qkv, attn, back_attn, logs, most, pairs - most, after(early, out_p, out_w)
        )
        keep_q, send_q = split_grad(place, h_one, back_qkv, False, "grad_qkv")
        got_q = swap(send_q, *CORE)
        far_p, near_w = after((far_p, near_w), send_q)
        sum_g = merged(
            add(keep_p[0, 0], got_p[0, 0], near_p[0], far_p), add(keep_w[0, 0], got_w[0, 0], far_w[0], near_w)
        )
        outs_g = [sum_g[k].astype(BF16) for k in range(4)]
        planes_g = [swap(outs_g[k], "shard", 2 * k) for k in range(1, 4)]

        got_q = after(got_q, outs_g)
        out_q = add(keep_q[:, 1], got_q[:, 1]).astype(BF16)
        near_q = swap(out_q, *X)
        token_grad, small = qkv_back(
            tokens, table, full_qkv, back_qkv, after(back_resid, outs_g, out_q), qkv_sums, mlp_sums, fc_sums
        )
        near_q = after(near_q, small)
        out_q = add(keep_q[1, 0], got_q[1, 0], near_q[1]).astype(BF16)
        far_q = swap(out_q, *Y)
        planes_g = after(planes_g, out_q)
        own_g = add(outs_g[0], *planes_g).astype(BF16)
        all_g = [own_g, swap(own_g, *X), swap(own_g, *Y), swap(own_g, "rep", 3)]
        far_q = after(far_q, own_g)

        sum_q = add(keep_q[0, 0], got_q[0, 0], near_q[0], far_q)
        sum_q = jnp.concatenate([sum_q, jnp.broadcast_to(small, (4, *small.shape))], axis=1)
        level_q = swap(sum_q[2:].astype(BF16), "shard", 4)
        level_q, all_g = after((level_q, all_g), sum_q)
        next_q = swap(add(sum_q[1], level_q[1]).astype(BF16), "shard", 2)
        own_q = add(sum_q[0], level_q[0], next_q).astype(BF16)
        all_q = [own_q, swap(own_q, *X), swap(own_q, *Y), swap(own_q, "rep", 3)]
        high = own // 2
        half = width // 2
        small = add(*[value[high:] for value in all_q])
        small = add(small, swap(small, *CORE)).reshape(-1)
        top, bottom = settle([value[:high] for value in all_q], across, along)
        grad_qkv = jnp.concatenate(
            [
                blocks_of(*[[piece[:, i * half : (i + 1) * half] for piece in line] for line in (top, bottom)])
                for i in range(3)
            ],
            axis=1,
        )
        half = w_fc.shape[1] // 2
        cuts = [0, width, 2 * width, 2 * width + half, own_g.shape[1]]
        settled = [
            settle([value[:, cuts[i] : cuts[i + 1]] for value in all_g], across, along) for i in range(4)
        ]
        (first_top, first_bottom), (second_top, second_bottom) = settled[:2]
        grad_proj = jnp.concatenate(
            [
                block
                for one, two in ((first_top, second_top), (first_bottom, second_bottom))
                for i in range(2)
                for block in (one[i], two[i])
            ],
            axis=0,
        ).astype(F32)
        grad_fc, grad_out = blocks_of(*settled[2]), blocks_of(*settled[3])
        one = [lax.dynamic_slice(small, (i * width + mine * own,), (own,)) for i in range(8)]
        fc_row = lax.dynamic_slice(small, (8 * width + mine * 4 * own,), (4 * own,))
    return (
        output,
        token_grad,
        one[0],
        one[1],
        grad_qkv,
        one[2],
        one[3],
        grad_out,
        one[4],
        one[5],
        one[6],
        grad_fc,
        fc_row,
        grad_proj,
        one[7],
    )


def solution(mesh):
    both = ("rep", "shard")
    matrix, vector = P("shard", None), P("shard")
    return jax.shard_map(
        local,
        mesh=mesh,
        in_specs=(
            P(both, None),
            P(both, None),
            P(both),
            P(both),
            vector,
            vector,
            matrix,
            vector,
            vector,
            matrix,
            vector,
            vector,
            vector,
            matrix,
            vector,
            matrix,
            vector,
        ),
        out_specs=(
            P(both, None),
            P(both, None),
            vector,
            vector,
            matrix,
            vector,
            vector,
            matrix,
            vector,
            vector,
            vector,
            matrix,
            vector,
            matrix,
            vector,
        ),
        check_vma=False,
    )
```
